512 devices in a mesh: seq: 64 (over z, x, core), head: 8 (over y).
Axes of the slice: x: 4, y: 8, z: 8, core: 2. Of those that a mesh axis runs over, the one named last changes fastest.
Arguments:
- loaded: bfloat16 [8192, 2048], P('seq', 'head'), may hold values from -6 to 6
- out_grad: bfloat16 [8192, 2048], P('seq', 'head'), may hold values from -6 to 6
- w_query: bfloat16 [2048, 2048], P(None, 'head'), may hold values from -0.125 to 0.125
- w_key: bfloat16 [2048, 2048], P(None, 'head'), may hold values from -0.125 to 0.125
- w_value: bfloat16 [2048, 2048], P(None, 'head'), may hold values from -0.125 to 0.125
- w_beta: bfloat16 [2048, 16], P(None, 'head'), may hold values from -0.125 to 0.125
- beta_max: float32 [16], P('head'), may hold values from 0.015625 to 1
- out_gain: float32 [128], replicated, may hold values from 0.1 to 1.9
- clip_lengths: int32 [16], replicated, may hold values from 1 to 2048, 8192 in all
- delay_offsets: int32 [4], replicated, may hold values from 0 to 3, each once
- block_order: int32 [64, 64], P('seq'), may hold values from 0 to 63, each once within a row
Outputs:
- head_out: bfloat16 [8192, 2048], P('seq', 'head')
- input_grad: bfloat16 [8192, 2048], P('seq', 'head')
The draws below stay inside these ranges and needn't reach their ends.
Inputs may be any that keep to these rules, and one draw needn't show every extreme that they name: `clip_lengths`: the clip lengths sum to 8192; the longest is exactly 2048. `delay_offsets`: each codebook has a different delay. `block_order`: each row is a permutation of 0 to 63.
All inputs are finite; a program needn't handle non-finite values.
Results may differ from the reference program's by a relative error of at most 0.022.
Values may be sent and summed in bfloat16 or wider, within the bound.
A program may use at most 128 MiB of HBM per device.

```python
import math
import jax
import jax.numpy as jnp
import numpy as np
from jax import lax

D = 2048
DK = 128
DV = 128
CODEBOOKS = 4
SPAN = 128
CLIPS = 16
TOK_DEV = 128
HEADS = 16
TOKENS = 8192
MOST = 2048
SOURCES = 64


def levels(stream_key, shape, split, least, high):
    factor_of, own = 1.0, jax.random.fold_in(stream_key, 6)
    for dim, blocks in split:
        heights = jnp.exp(jax.random.uniform(jax.random.fold_in(own, dim), (blocks,), jnp.float32, least / len(split), high / len(split)))
        factor_of = factor_of * jnp.repeat(heights, shape[dim] // blocks).reshape([-1 if axis == dim else 1 for axis in range(len(shape))])
    return factor_of


def profile(amount, total, bound, lean):
    weights = [(1 << 20) // math.isqrt(grade ** lean) + 1 for grade in range(2, amount + 1)]
    rest, given = total - bound - (amount - 1), [1] * (amount - 1)
    while rest > 0:
        movable = [i for i in range(amount - 1) if given[i] < bound]
        whole, budget = sum([weights[i] for i in movable]), rest
        for i in movable:
            addition = min(bound - given[i], max(1, budget * weights[i] // whole), rest)
            given[i] = given[i] + addition
            rest = rest - addition
    return np.array([bound] + given)


def uneven_parts(rng, number_of, total, most, lean):
    if number_of == 2:
        one = jax.random.randint(rng, (), max(1, total - most), min(most, total - 1) + 1)
        return jnp.stack([one, total - one])
    tallies = jnp.asarray(profile(number_of, total, most, lean), jnp.int32)
    couples = (number_of - 1) // 2
    giver, taker = tallies[1:1 + 2 * couples:2], tallies[2:2 + 2 * couples:2]
    slack = jnp.minimum(giver - 1, most - taker)
    moved = jax.random.randint(jax.random.fold_in(rng, 1), (couples,), 0, 1 << 20) % (slack + 1)
    tallies = tallies.at[1:1 + 2 * couples:2].set(giver - moved).at[2:2 + 2 * couples:2].set(taker + moved)
    return tallies[jax.random.permutation(jax.random.fold_in(rng, 2), number_of)]


def noise(own_key, dims, scale, most, cuts=(), kind=jnp.bfloat16):
    loudness = levels(own_key, dims, cuts, -0.22, 0.18) if cuts else 1.0
    values = jax.random.normal(own_key, dims, jnp.float32) * scale * loudness
    return jnp.minimum(jnp.maximum(values, -most), most).astype(kind)


def setup_inputs(seed: int = 0) -> dict:
    key_of = jax.random.split(jax.random.key(seed), 12)
    return {
        "loaded": noise(key_of[0], (TOKENS, D), 1.0, 6.0, ((0, 64), (1, 8))),
        "out_grad": noise(key_of[1], (TOKENS, HEADS * DV), 1.0, 6.0, ((0, 64), (1, 8))),
        "w_query": noise(key_of[2], (D, HEADS * DK), D ** -0.5, 0.125, ((1, 8),)),
        "w_key": noise(key_of[3], (D, HEADS * DK), D ** -0.5, 0.125, ((1, 8),)),
        "w_value": noise(key_of[4], (D, HEADS * DV), D ** -0.5, 0.125, ((1, 8),)),
        "w_beta": noise(key_of[5], (D, HEADS), D ** -0.5, 0.125, ((1, 8),)),
        "beta_max": jnp.clip(jnp.exp(math.log(1.0) - 4.158883 * jax.random.uniform(key_of[6], (HEADS,), jnp.float32) ** levels(key_of[6], (HEADS,), ((0, 8),), -0.2, 0.2)), 0.015625, 1.0),
        "out_gain": jnp.clip(1.0 + 0.18 * jax.random.normal(key_of[7], (DV,), jnp.float32), 0.1, 1.9),
        "clip_lengths": uneven_parts(key_of[8], CLIPS, TOKENS, MOST, 2).astype(jnp.int32),
        "delay_offsets": jax.random.permutation(key_of[9], CODEBOOKS).astype(jnp.int32),
        "block_order": jax.vmap(lambda own: jax.random.permutation(own, SOURCES))(jax.random.split(key_of[10], SOURCES)).reshape((SOURCES, SOURCES)).astype(jnp.int32),
    }


EPSILON = 1e-06
HIGHEST = lax.Precision.HIGHEST

def clip_start(clip_lengths, positions):
    clip_ends = jnp.cumsum(clip_lengths).astype(jnp.int32)
    finished = clip_ends[None, :] <= positions[:, None]
    return lax.optimization_barrier(jnp.sum(jnp.where(finished, clip_lengths[None, :], 0), axis=1)).astype(jnp.int32)

def column_delays(delay_offsets, columns, group_width):
    codebook = columns // group_width
    matches = codebook[:, None] == jnp.arange(delay_offsets.shape[0], dtype=jnp.int32)[None, :]
    return lax.optimization_barrier(jnp.sum(jnp.where(matches, delay_offsets[None, :], 0), axis=1)).astype(jnp.int32)

def prepare(q_raw, k_raw, logit, rate_cap):
    query_rows = q_raw / jnp.sqrt(lax.optimization_barrier(jnp.sum(q_raw * q_raw, axis=-1, keepdims=True)) + EPSILON)
    key_rows = k_raw / jnp.sqrt(lax.optimization_barrier(jnp.sum(k_raw * k_raw, axis=-1, keepdims=True)) + EPSILON)
    beta_rate = rate_cap * jax.nn.sigmoid(logit[:, 0])
    return (query_rows, key_rows, beta_rate)

def span_terms(key_rows, value_rows, beta_rate, clip_begin, span_first):
    span_len = key_rows.shape[0]
    key_width = key_rows.shape[1]
    same_clip = (clip_begin[:, None] == clip_begin[None, :]).astype(jnp.float32)
    gram = beta_rate[:, None] * jnp.dot(key_rows, key_rows.T, precision=HIGHEST) * same_clip
    system = jnp.eye(span_len, dtype=jnp.float32) + jnp.tril(gram, -1)
    stacked = beta_rate[:, None] * jnp.concatenate([key_rows, value_rows], axis=1)
    solved = jax.scipy.linalg.solve_triangular(system, stacked, lower=True, unit_diagonal=True)
    carried = (clip_begin < span_first).astype(jnp.float32)
    final_mask = (clip_begin == clip_begin[-1]).astype(jnp.float32)
    return (solved[:, :key_width], solved[:, key_width:], carried, final_mask, same_clip)

def span_output(state_in, pieces):
    query_rows, key_rows, value_rows, beta_rate, clip_begin, span_first = pieces
    key_part, value_part, carried, final_mask, same_clip = span_terms(key_rows, value_rows, beta_rate, clip_begin, span_first)
    refreshed = value_part - carried[:, None] * jnp.dot(key_part, state_in, precision=HIGHEST)
    scores = jnp.tril(jnp.dot(query_rows, key_rows.T, precision=HIGHEST)) * same_clip
    outputs = carried[:, None] * jnp.dot(query_rows, state_in, precision=HIGHEST) + jnp.dot(scores, refreshed, precision=HIGHEST)
    state_out = carried[-1] * state_in + jnp.dot(key_rows.T, final_mask[:, None] * refreshed, precision=HIGHEST)
    return (state_out, outputs)

def run_head(q_raw, k_raw, v_raw, logit, rate_cap, out_gain, clip_begin, positions, state_in):
    query_rows, key_rows, beta_rate = prepare(q_raw, k_raw, logit, rate_cap)
    span_count = q_raw.shape[0] // SPAN
    pieces = (query_rows.reshape(span_count, SPAN, -1), key_rows.reshape(span_count, SPAN, -1), v_raw.reshape(span_count, SPAN, -1), beta_rate.reshape(span_count, SPAN), clip_begin.reshape(span_count, SPAN), positions.reshape(span_count, SPAN)[:, 0])
    state_out, outputs = lax.scan(span_output, state_in, pieces)
    raw_out = outputs.reshape(-1, outputs.shape[-1])
    normed = raw_out / jnp.sqrt(lax.optimization_barrier(jnp.mean(raw_out * raw_out, axis=-1, keepdims=True)) + EPSILON) * out_gain[None, :]
    return (normed, state_out)

def back_product(gradient, weight):
    return lax.dot_general(gradient.astype(jnp.float32), weight.astype(jnp.float32), (((1,), (1,)), ((), ())), preferred_element_type=jnp.float32)

def reference(loaded, out_grad, w_query, w_key, w_value, w_beta, beta_max, out_gain, clip_lengths, delay_offsets, block_order):
    sources = block_order.shape[0]
    block_rows = TOK_DEV // sources
    blocks = loaded.reshape(sources, sources, block_rows, D).transpose(1, 0, 2, 3)
    inverse = jnp.argsort(block_order, axis=1).astype(jnp.int32)
    arranged = jnp.take_along_axis(blocks, inverse[:, :, None, None], axis=1).reshape(TOKENS, D)
    positions = jnp.arange(TOKENS, dtype=jnp.int32)
    clip_begin = clip_start(clip_lengths, positions)
    col_delay = column_delays(delay_offsets, jnp.arange(D, dtype=jnp.int32), D // CODEBOOKS)
    delayed = jnp.zeros((TOKENS, D), jnp.bfloat16)
    for shift_by in range(CODEBOOKS):
        shifted = jnp.concatenate([jnp.zeros((shift_by, D), jnp.bfloat16), arranged[:TOKENS - shift_by]], axis=0)
        inside = positions - shift_by >= clip_begin
        delayed = jnp.where((col_delay[None, :] == shift_by) & inside[:, None], shifted, delayed)

    def one_head(summed, head_index):
        wq_head = lax.dynamic_slice_in_dim(w_query, head_index * DK, DK, 1)
        wk_head = lax.dynamic_slice_in_dim(w_key, head_index * DK, DK, 1)
        wv_head = lax.dynamic_slice_in_dim(w_value, head_index * DV, DV, 1)
        wb_head = lax.dynamic_slice_in_dim(w_beta, head_index, 1, 1)
        q_raw = jnp.dot(delayed.astype(jnp.float32), wq_head.astype(jnp.float32), preferred_element_type=jnp.float32)
        k_raw = jnp.dot(delayed.astype(jnp.float32), wk_head.astype(jnp.float32), preferred_element_type=jnp.float32)
        v_raw = jnp.dot(delayed.astype(jnp.float32), wv_head.astype(jnp.float32), preferred_element_type=jnp.float32)
        logit = jnp.dot(delayed.astype(jnp.float32), wb_head.astype(jnp.float32), preferred_element_type=jnp.float32)
        rate_cap = lax.dynamic_index_in_dim(beta_max, head_index, keepdims=False)

        def forward(query_in, key_in, value_in, logit_in):
            start_state = jnp.zeros((DK, DV), jnp.float32)
            return run_head(query_in, key_in, value_in, logit_in, rate_cap, out_gain, clip_begin, positions, start_state)[0]
        normed, pullback = jax.vjp(forward, q_raw, k_raw, v_raw, logit)
        cotangent = lax.dynamic_slice_in_dim(out_grad, head_index * DV, DV, 1).astype(jnp.float32)
        gradients = [grad_part.astype(jnp.bfloat16) for grad_part in pullback(cotangent)]
        backward = back_product(gradients[0], wq_head) + back_product(gradients[1], wk_head)
        backward = backward + back_product(gradients[2], wv_head) + back_product(gradients[3], wb_head)
        return (summed + backward, normed.astype(jnp.bfloat16))
    summed, outputs = lax.scan(one_head, jnp.zeros((TOKENS, D), jnp.float32), jnp.arange(HEADS, dtype=jnp.int32))
    head_out = outputs.transpose(1, 0, 2).reshape(TOKENS, HEADS * DV)
    delayed_grad = summed.astype(jnp.bfloat16)
    input_grad = jnp.zeros((TOKENS, D), jnp.bfloat16)
    for shift_by in range(CODEBOOKS):
        ahead = jnp.concatenate([delayed_grad[shift_by:], jnp.zeros((shift_by, D), jnp.bfloat16)], axis=0)
        inside = (positions + shift_by < TOKENS) & (clip_start(clip_lengths, positions + shift_by) <= positions)
        input_grad = jnp.where((col_delay[None, :] == shift_by) & inside[:, None], ahead, input_grad)
    return (head_out, input_grad)
```

```python
import functools

import jax
import jax.numpy as jnp
from jax import lax
from jax.experimental import pallas as pl
from jax.experimental.pallas import tpu as pltpu
from jax.sharding import PartitionSpec as P

EPSILON = 1e-06
F32, BF16 = jnp.float32, jnp.bfloat16
CORES = 2
CHIPS_X = 4

NN = (1, 0)
NT = (1, 1)
TN = (0, 0)


def dot(a, b, kind=NN):
    return lax.dot_general(
        a, b, (((kind[0],), (kind[1],)), ((), ())), preferred_element_type=F32
    )


def split(x):
    high = x.astype(BF16)
    return high, (x - high.astype(F32)).astype(BF16)


def mm3(a, b, kind=NN):
    ah, al = split(a)
    bh, bl = split(b)
    return dot(
        jnp.concatenate([ah, ah, al], axis=kind[0]),
        jnp.concatenate([bh, bl, bh], axis=kind[1]),
        kind,
    )


def mm2(a, b, kind=NN):
    bh, bl = split(b)
    return dot(
        jnp.concatenate([a, a], axis=kind[0]), jnp.concatenate([bh, bl], axis=kind[1]), kind
    )


def mm1(a, b, kind=NN):
    return dot(a.astype(BF16), b.astype(BF16), kind)


def one_hot(condition):
    return jnp.where(condition, 1.0, 0.0).astype(BF16)


def iota(shape, dim):
    return lax.broadcasted_iota(jnp.int32, shape, dim)


def clip_start(lengths, positions):
    begin = jnp.zeros_like(positions)
    end = jnp.int32(0)
    for c in range(lengths.shape[0]):
        size = lengths[c]
        end = end + size
        begin = begin + jnp.where(end <= positions, size, 0)
    return begin


def kernel(
    dims,
    loaded,
    out_grad,
    w_query,
    w_key,
    w_value,
    w_beta,
    beta_max,
    out_gain,
    clip_lengths,
    delay_offsets,
    block_order,
    head_out,
    input_grad,
    wq,
    wk,
    wv,
    cot,
    r1,
    s2,
    r2,
    arranged,
    tail,
    feat,
    acc,
    ab,
    sib_ab,
    plane,
    group,
    from_z1,
    from_z2,
    a_next,
    states,
    grads,
    sib_grad,
    gplane,
    ggroup,
    gz1,
    gz2,
    dstates,
    gcat,
    rs_send,
    rs_recv,
    summed,
    follow,
    give_s,
    give_d,
    local_sem,
    send_sem,
    recv_sem,
):
    Z, X, H, F, W = dims["Z"], dims["X"], dims["H"], dims["F"], dims["W"]
    C = CORES
    G = X * C
    S = Z * G
    BR = F // S
    N = 128
    CB = delay_offsets.shape[0]
    seq, y = lax.axis_index("seq"), lax.axis_index("head")
    z = lax.div(seq, G)
    g = lax.rem(seq, G)
    x = lax.div(g, C)
    core = lax.rem(g, C)
    other = 1 - core

    def at(zz, gg):
        return (zz * G + gg, y)

    counter = [0]
    started = []

    def remote(src, dst, device, index=None):
        if index is None:
            index = counter[0]
            counter[0] += 1
        return pltpu.make_async_remote_copy(
            src_ref=src,
            dst_ref=dst,
            send_sem=send_sem.at[index],
            recv_sem=recv_sem.at[index],
            device_id=device,
            device_id_type=pl.DeviceIdType.MESH,
        )

    def go(copy):
        copy.start()
        started.append(copy)
        return copy

    fetches = [
        pltpu.make_async_copy(src, dst, local_sem.at[i])
        for i, (src, dst) in enumerate(
            ((w_query, wq), (w_key, wk), (w_value, wv), (out_grad, cot))
        )
    ]
    for copy in fetches:
        copy.start()

    partners = [at(lax.rem(z + k, Z), g) for k in range(1, Z)]
    partners += [at(z, lax.rem(g + k, G)) for k in range(1, G)]
    partners += [(lax.rem(seq + 1, S), y), (lax.rem(seq + S - 1, S), y)]
    partners += [(seq, lax.rem(y + 1, H)), (seq, lax.rem(y + H - 1, H))]
    barrier = pltpu.get_barrier_semaphore()
    for partner in partners:
        pl.semaphore_signal(barrier, inc=1, device_id=partner, device_id_type=pl.DeviceIdType.MESH)
    pl.semaphore_wait(barrier, len(partners))

    rows1 = G * BR
    copies = []
    for k in range(1, Z):
        to = lax.rem(z + k, Z)
        src = loaded.at[pl.ds(pl.multiple_of(to * rows1, rows1), rows1)]
        copies.append(go(remote(src, r1.at[z], at(to, g))))
    r1[z] = loaded[pl.ds(pl.multiple_of(z * rows1, rows1), rows1), :]

    first = seq * F
    pos_col = first + iota((F, 1), 0)
    begin_col = clip_start(clip_lengths, pos_col)
    begin_row = clip_start(clip_lengths, first + iota((1, F), 1))
    delay = delay_offsets[lax.div(y * CB, H)]
    row, col = iota((F, F), 0), iota((F, F), 1)
    same = jnp.where(begin_col == begin_row, 1.0, 0.0)
    low = jnp.where(row > col, same, 0.0)
    low_eq = jnp.where(row >= col, same, 0.0)
    eye = jnp.where(row == col, 1.0, 0.0)
    carried = jnp.where(begin_col < first, 1.0, 0.0)
    final = jnp.where(begin_col == begin_col[F - 1 : F, :], 1.0, 0.0)
    carried_last = carried[F - 1 : F, :]

    zbr = Z * BR
    to_g, to_z, to_r = row // zbr, (row % zbr) // BR, row % BR
    regroup = one_hot(col == to_z * rows1 + to_g * BR + to_r)
    order = jnp.broadcast_to(block_order[...], (16, S)).astype(F32).astype(BF16)
    src_i, out_q = iota((S, F), 0), iota((S, F), 1)
    spread = one_hot(src_i == ((out_q % zbr) // BR) * G + out_q // zbr)
    target = dot(order, spread)[0:1, :].astype(jnp.int32) * BR + iota((1, F), 1) % BR
    place = one_hot(row == target)

    for copy in copies:
        copy.wait_recv()
    s2[...] = dot(regroup, r1[...].reshape(F, W)).astype(BF16).reshape(G, zbr, W)
    copies = []
    for k in range(1, G):
        to = lax.rem(g + k, G)
        copies.append(go(remote(s2.at[to], r2.at[g], at(z, to))))
    r2[g] = s2[g]
    for copy in copies:
        copy.wait_recv()
    arranged[...] = dot(place, r2[...].reshape(F, W)).astype(BF16)

    halo = go(remote(arranged.at[pl.ds(F - 16, 16)], tail, (lax.rem(seq + 1, S), y)))
    half = F // 2
    halves = (half, 0)

    def delayed_rows(start, source_first, source_count):
        frames = first + start + iota((half, 1), 0)
        wanted = jnp.where(frames - delay >= begin_col[start : start + half, :], frames - delay, -100)
        return one_hot(wanted == first + source_first + iota((half, source_count), 1))

    up, down = (seq, lax.rem(y + 1, H)), (seq, lax.rem(y + H - 1, H))
    hops = (H // 2, H - 1 - H // 2)
    sign = (-1, 1)
    gathers = {}
    for d in range(2):
        for s in range(hops[d]):
            for b in range(2):
                owner = lax.rem(y + sign[d] * s + H, H)
                part = feat.at[owner, pl.ds(halves[b], half)]
                gathers[d, s, b] = remote(part, part, (up, down)[d])

    feat[y, half:F, :] = dot(delayed_rows(half, 0, F), arranged[...]).astype(BF16)
    for d in range(2):
        if hops[d]:
            go(gathers[d, 0, 0])
    halo.wait_recv()
    both = jnp.concatenate([tail[...], arranged[...]], axis=0)
    feat[y, 0:half, :] = dot(delayed_rows(0, -16, F + 16), both).astype(BF16)
    for d in range(2):
        if hops[d]:
            go(gathers[d, 0, 1])

    def project(owner, begin):
        block = feat[owner]
        here = pl.ds(pl.multiple_of(owner * W, W), W)
        for i, weight in enumerate((wq, wk, wv)):
            value = dot(block, weight[here, :])
            at_cols = slice(i * W, (i + 1) * W)
            acc[:, at_cols] = value if begin else acc[:, at_cols] + value
        value = dot(block, w_beta[:, here], NT)
        acc[:, 3 * W : 3 * W + 16] = value if begin else acc[:, 3 * W : 3 * W + 16] + value

    for copy in fetches:
        copy.wait()
    project(y, True)
    for s in range(hops[0]):
        for b in range(2):
            for d in range(2):
                if s < hops[d]:
                    gathers[d, s, b].wait_recv()
                    if s + 1 < hops[d]:
                        go(gathers[d, s + 1, b])
        for d in range(2):
            if s < hops[d]:
                project(lax.rem(y + sign[d] * (s + 1) + H, H), False)

    heads = range(2)
    Q, K, V, beta, nq, nk, sig, Gm, T = ({} for _ in range(9))
    for h in heads:
        cols = slice(h * N, (h + 1) * N)
        q_raw, k_raw = acc[:, cols], acc[:, W + h * N : W + (h + 1) * N]
        V[h] = acc[:, 2 * W + h * N : 2 * W + (h + 1) * N]
        nq[h] = lax.rsqrt(jnp.sum(q_raw * q_raw, axis=1, keepdims=True) + EPSILON)
        nk[h] = lax.rsqrt(jnp.sum(k_raw * k_raw, axis=1, keepdims=True) + EPSILON)
        Q[h], K[h] = q_raw * nq[h], k_raw * nk[h]
        sig[h] = 1.0 / (1.0 + jnp.exp(-acc[:, 3 * W + h : 3 * W + h + 1]))
        beta[h] = beta_max[h] * sig[h]
    L = {}
    for h in heads:
        Gm[h] = mm3(K[h], K[h], NT) * low
        L[h] = beta[h] * Gm[h]
    size = 1
    while size < F:
        pair = (
            ((row // (2 * size)) == (col // (2 * size)))
            & ((row // size) % 2 == 1)
            & ((col // size) % 2 == 0)
        )
        inner = {h: jnp.where(pair, L[h], 0.0) for h in heads}
        if size == 1:
            T = {h: eye - inner[h] for h in heads}
        else:
            half_way = {h: mm3(T[h], inner[h]) for h in heads}
            T = {h: T[h] - mm3(half_way[h], T[h]) for h in heads}
        size *= 2
    Wk, Wv = {}, {}
    for h in heads:
        both = mm3(T[h], beta[h] * jnp.concatenate([K[h], V[h]], axis=1))
        Wk[h], Wv[h] = both[:, :N], both[:, N:]
    for h in heads:
        both = mm3(K[h], jnp.concatenate([Wk[h], final * Wv[h]], axis=1), TN)
        ab[h, :, :N] = carried_last * (eye - both[:, :N])
        ab[h, :, N:] = both[:, N:]

    sibling = at(z, x * C + other)
    copy = go(remote(ab.at[other], sib_ab, sibling))
    P_, Oloc, R = {}, {}, {}
    for h in heads:
        P_[h] = mm3(Q[h], K[h], NT) * low_eq
        both = mm3(P_[h], jnp.concatenate([carried * Wk[h], Wv[h]], axis=1))
        R[h] = carried * Q[h] - both[:, :N]
        Oloc[h] = both[:, N:]
    copy.wait_recv()
    own, sib = ab[core], sib_ab[...]
    early = jnp.where(core == 0, own, sib)
    late = jnp.where(core == 0, sib, own)
    a_early, b_early = early[:, :N], early[:, N:]
    a_late, b_late = late[:, :N], late[:, N:]
    zero = jnp.zeros((N, N), F32)
    pad_b = jnp.concatenate([zero, b_late], axis=1)
    plane[x] = (mm3(a_late, early) + pad_b).astype(BF16)
    copies = []
    for k in range(1, X):
        to = lax.rem(x + k, X)
        copies.append(go(remote(plane.at[x], plane.at[x], at(z, to * C + core))))
    for copy in copies:
        copy.wait_recv()

    def then(before, after):
        shift = jnp.concatenate([zero, after[:, N:].astype(F32)], axis=1)
        return mm2(after[:, :N], before) + shift

    def then32(before, after):
        shift = jnp.concatenate([zero, after[:, N:]], axis=1)
        return mm3(after[:, :N], before) + shift

    maps = [plane[i] for i in range(X)]
    identity = jnp.concatenate([eye, zero], axis=1)
    prefix = [identity, maps[0].astype(F32)]
    if X == 4:
        front = then(prefix[1], maps[1])
        back = then(maps[2].astype(F32), maps[3])
        total = then32(front, back)
        prefix += [front]
    else:
        for i in range(1, X):
            total = then(prefix[-1], maps[i])
            prefix.append(total)
    group[...] = total.astype(BF16)
    z1, z2 = lax.rem(z + 1, Z), lax.rem(z + 2, Z)
    y1, y2 = lax.rem(z + Z - 1, Z), lax.rem(z + Z - 2, Z)
    copies = [
        go(remote(group, from_z1, at(z1, g))),
        go(remote(group.at[:, pl.ds(N, N)], from_z2, at(z2, g))),
    ]
    next_copy = go(remote(group.at[:, pl.ds(0, N)], a_next, at(y1, g)))
    if X == 4:
        prefix.append(then(front, maps[2]))
        a1, a2, a3 = (maps[i][:, :N] for i in (1, 2, 3))
        suffix = [mm2(a3, mm2(a2, a1.astype(F32))), back[:, :N], a3.astype(F32), eye]
    else:
        suffix = [eye]
        for i in range(X - 1, 0, -1):
            suffix.insert(0, mm3(suffix[0], maps[i][:, :N].astype(F32)))

    def pick(options, index):
        value = options[0]
        for i in range(1, len(options)):
            value = jnp.where(index == i, options[i], value)
        return value

    before_me = pick(prefix[:X], x)
    after_me = pick(suffix, x)
    for copy in copies:
        copy.wait_recv()
    s_group = from_z1[:, N:].astype(F32) + dot(from_z1[:, :N], from_z2[...])
    s_chip = before_me[:, N:] + mm3(before_me[:, :N], s_group)
    s_late = b_early + mm3(a_early, s_chip)
    states[core] = jnp.where(core == 0, s_chip, s_late)
    give_s[...] = jnp.where(core == 0, s_late, s_chip)
    go(remote(give_s, states.at[core], sibling)).wait_recv()

    gain = out_gain[...]
    O, dO = {}, {}
    for h in heads:
        cols = slice(h * N, (h + 1) * N)
        O[h] = Oloc[h] + mm3(R[h], states[h])
        inv = lax.rsqrt(jnp.mean(O[h] * O[h], axis=1, keepdims=True) + EPSILON)
        head_out[:, cols] = (O[h] * inv * gain).astype(BF16)
        scaled = cot[:, cols].astype(F32) * gain
        unit = O[h] * inv
        dO[h] = inv * (scaled - unit * jnp.mean(scaled * unit, axis=1, keepdims=True))
        grads[h] = mm3(R[h], dO[h], TN)
    copy = go(remote(grads.at[other], sib_grad, sibling))
    U, dU0, Y, dX0, dP, dQ, dK0, Zv = ({} for _ in range(8))
    for h in heads:
        S0 = states[h]
        KS = carried * mm3(K[h], S0)
        Zv[h] = V[h] - KS
        U[h] = Wv[h] - carried * mm3(Wk[h], S0)
    copy.wait_recv()
    own, sib = grads[core], sib_grad[...]
    g_early = jnp.where(core == 0, own, sib)
    g_late = jnp.where(core == 0, sib, own)
    gplane[x] = (g_early + mm3(a_early, g_late, TN)).astype(BF16)
    copies = []
    for k in range(1, X):
        to = lax.rem(x + k, X)
        copies.append(go(remote(gplane.at[x], gplane.at[x], at(z, to * C + core))))
    for h in heads:
        dU0[h] = mm3(P_[h], dO[h], TN)
        both = mm3(T[h], jnp.concatenate([dU0[h], final * K[h]], axis=1), TN)
        dX0[h], Y[h] = both[:, :N], both[:, N:]
    for copy in copies:
        copy.wait_recv()
    gs = [gplane[i].astype(F32) for i in range(X)]

    def back_through(i, later):
        return gs[i] + mm2(maps[i][:, :N], later, TN)

    if X == 4:
        pair_late = back_through(2, gs[3])
        pair_early = back_through(0, gs[1])
        g_total = pair_early + mm3(front[:, :N], pair_late, TN)
        behind = [back_through(1, pair_late), pair_late, gs[3], zero]
    else:
        behind = [zero]
        for i in range(X - 1, -1, -1):
            behind.insert(0, back_through(i, behind[0]))
        g_total = behind[0]
        behind = behind[1:]
    ggroup[...] = g_total.astype(BF16)
    copies = [
        go(remote(ggroup, gz1, at(y1, g))),
        go(remote(ggroup, gz2, at(y2, g))),
    ]
    behind_me = pick(behind, x)
    for h in heads:
        S0 = states[h]
        dP[h] = mm3(dO[h], U[h], NT) * low_eq
        dQ[h] = carried * mm3(dO[h], S0, NT) + mm3(dP[h], K[h])
        dK0[h] = mm3(dP[h], Q[h], TN)
        grad = nq[h] * (dQ[h] - Q[h] * jnp.sum(Q[h] * dQ[h], axis=1, keepdims=True))
        gcat[:, h * N : (h + 1) * N] = grad.astype(BF16)
    next_copy.wait_recv()
    for copy in copies:
        copy.wait_recv()
    d_group = gz1[...].astype(F32) + dot(a_next[...], gz2[...], TN)
    d_chip = behind_me + mm3(after_me, d_group, TN)
    d_early = g_late + mm3(a_late, d_chip, TN)
    dstates[core] = jnp.where(core == 0, d_early, d_chip)
    give_d[...] = jnp.where(core == 0, d_chip, d_early)
    go(remote(give_d, dstates.at[core], sibling)).wait_recv()

    dlog = jnp.zeros((F, 16), F32)
    for h in heads:
        S0, dS = states[h], dstates[h]
        dX = dX0[h] + mm3(Y[h], dS)
        scaled = beta[h] * dX
        both = mm3(dX, jnp.concatenate([U[h], S0], axis=0), NT)
        dL = -both[:, :F] * low
        dG = beta[h] * dL
        dK = dK0[h] + mm3(final * U[h], dS, NT)
        dK = dK - carried * beta[h] * both[:, F:]
        dK = dK + mm3(dG, K[h]) + mm3(dG, K[h], TN)
        d_beta = jnp.sum(dX * Zv[h], axis=1, keepdims=True)
        d_beta = d_beta + jnp.sum(dL * Gm[h], axis=1, keepdims=True)
        grad = nk[h] * (dK - K[h] * jnp.sum(K[h] * dK, axis=1, keepdims=True))
        gcat[:, W + h * N : W + (h + 1) * N] = grad.astype(BF16)
        gcat[:, 2 * W + h * N : 2 * W + (h + 1) * N] = scaled.astype(BF16)
        d_logit = d_beta * beta[h] * (1.0 - sig[h])
        dlog = dlog + jnp.where(iota((F, 16), 1) == h, d_logit, 0.0)
    dlog = dlog.astype(BF16)

    def partial(owner):
        here = pl.ds(pl.multiple_of(owner * W, W), W)
        value = dot(dlog, w_beta[:, here])
        for i, weight in enumerate((wq, wk, wv)):
            value = value + dot(gcat[:, i * W : (i + 1) * W], weight[here, :], NT)
        return value

    base = (0, hops[0])
    reduces = {}
    for d in range(2):
        for s in range(hops[d]):
            for b in range(2):
                slot = base[d] + s
                reduces[d, s, b] = remote(
                    rs_send.at[slot, b], rs_recv.at[slot, b], (up, down)[d]
                )
    for s in range(hops[0]):
        values = {}
        for d in range(2):
            if s < hops[d]:
                owner = y + hops[0] - s if d == 0 else y - hops[1] + s + H
                values[d] = partial(lax.rem(owner, H))
        for b in range(2):
            for d in range(2):
                if s < hops[d]:
                    slot = base[d] + s
                    value = values[d][b * half : (b + 1) * half, :]
                    if s:
                        reduces[d, s - 1, b].wait_recv()
                        value = value + rs_recv[slot - 1, b].astype(F32)
                    rs_send[slot, b] = value.astype(BF16)
                    go(reduces[d, s, b])
    mine = partial(y)
    for b in range(2):
        value = mine[b * half : (b + 1) * half, :]
        for d in range(2):
            if hops[d]:
                reduces[d, hops[d] - 1, b].wait_recv()
                value = value + rs_recv[base[d] + hops[d] - 1, b].astype(F32)
        summed[b * half : (b + 1) * half, :] = value.astype(BF16)
        if b == 0:
            halo = go(remote(summed.at[pl.ds(0, 16)], follow, (lax.rem(seq + S - 1, S), y)))
    ahead = pos_col + delay
    reaches = (ahead < S * F) & (clip_start(clip_lengths, ahead) <= pos_col)
    wanted = jnp.where(reaches, ahead - first, -1)
    pull = one_hot(wanted == iota((F, F + 16), 1))
    halo.wait_recv()
    both = jnp.concatenate([summed[...], follow[...]], axis=0)
    input_grad[...] = dot(pull, both).astype(BF16)
    for copy in started:
        copy.wait_send()


def on_device(
    dims,
    loaded,
    out_grad,
    w_query,
    w_key,
    w_value,
    w_beta,
    beta_max,
    out_gain,
    clip_lengths,
    delay_offsets,
    block_order,
):
    Z, X, H = dims["Z"], dims["X"], dims["H"]
    F, W = dims["F"], dims["W"]
    G = X * CORES
    BR = F // (Z * G)
    N = 128
    half = F // 2
    hops = H - 1
    count = 128
    vmem, smem, anyw = (
        pl.BlockSpec(memory_space=s) for s in (pltpu.VMEM, pltpu.SMEM, pl.ANY)
    )
    D = w_query.shape[0]
    scratch = [
        pltpu.VMEM((D, W), BF16),
        pltpu.VMEM((D, W), BF16),
        pltpu.VMEM((D, W), BF16),
        pltpu.VMEM((F, W), BF16),
        pltpu.VMEM((Z, G * BR, W), BF16),
        pltpu.VMEM((G, Z * BR, W), BF16),
        pltpu.VMEM((G, Z * BR, W), BF16),
        pltpu.VMEM((F, W), BF16),
        pltpu.VMEM((16, W), BF16),
        pltpu.VMEM((H, F, W), BF16),
        pltpu.VMEM((F, 3 * W + 128), F32),
        pltpu.VMEM((2, N, 2 * N), F32),
        pltpu.VMEM((N, 2 * N), F32),
        pltpu.VMEM((X, N, 2 * N), BF16),
        pltpu.VMEM((N, 2 * N), BF16),
        pltpu.VMEM((N, 2 * N), BF16),
        pltpu.VMEM((N, N), BF16),
        pltpu.VMEM((N, N), BF16),
        pltpu.VMEM((2, N, N), F32),
        pltpu.VMEM((2, N, N), F32),
        pltpu.VMEM((N, N), F32),
        pltpu.VMEM((X, N, N), BF16),
        pltpu.VMEM((N, N), BF16),
        pltpu.VMEM((N, N), BF16),
        pltpu.VMEM((N, N), BF16),
        pltpu.VMEM((2, N, N), F32),
        pltpu.VMEM((F, 3 * W), BF16),
        pltpu.VMEM((hops, 2, half, W), BF16),
        pltpu.VMEM((hops, 2, half, W), BF16),
        pltpu.VMEM((F, W), BF16),
        pltpu.VMEM((16, W), BF16),
        pltpu.VMEM((N, N), F32),
        pltpu.VMEM((N, N), F32),
        pltpu.SemaphoreType.DMA((4,)),
        pltpu.SemaphoreType.DMA((count,)),
        pltpu.SemaphoreType.DMA((count,)),
    ]
    wide_beta = jnp.pad(w_beta.T, ((0, 14), (0, 0)))
    return pl.pallas_call(
        functools.partial(kernel, dims),
        out_shape=(
            jax.ShapeDtypeStruct((F, W), BF16),
            jax.ShapeDtypeStruct((F, W), BF16),
        ),
        in_specs=[vmem, anyw, anyw, anyw, anyw, vmem, smem, vmem, smem, smem, vmem],
        out_specs=(vmem, vmem),
        scratch_shapes=scratch,
        compiler_params=pltpu.CompilerParams(
            collective_id=0, has_side_effects=True, vmem_limit_bytes=40 * 2**20
        ),
    )(
        loaded,
        out_grad,
        w_query,
        w_key,
        w_value,
        wide_beta,
        beta_max,
        out_gain.reshape(1, -1),
        clip_lengths,
        delay_offsets,
        block_order,
    )


def build(mesh, chips_x, frames):
    seq, head = mesh.shape["seq"], mesh.shape["head"]
    dims = dict(Z=seq // (chips_x * CORES), X=chips_x, H=head, F=frames, W=256)
    return jax.shard_map(
        functools.partial(on_device, dims),
        mesh=mesh,
        in_specs=(
            P("seq", "head"),
            P("seq", "head"),
            P(None, "head"),
            P(None, "head"),
            P(None, "head"),
            P(None, "head"),
            P("head"),
            P(),
            P(),
            P(),
            P("seq", None),
        ),
        out_specs=(P("seq", "head"), P("seq", "head")),
        check_vma=False,
    )


def solution(mesh):
    return build(mesh, CHIPS_X, 128)
```

```python
import functools

import jax
import jax.numpy as jnp
from jax import lax
from jax.experimental import pallas as pl
from jax.experimental.pallas import tpu as pltpu
from jax.sharding import PartitionSpec as P

EPSILON = 1e-06
F32, BF16 = jnp.float32, jnp.bfloat16
CORES = 2
CHIPS_X = 4

NN = (1, 0)
NT = (1, 1)
TN = (0, 0)


def dot(a, b, kind=NN):
    return lax.dot_general(
        a, b, (((kind[0],), (kind[1],)), ((), ())), preferred_element_type=F32
    )


def split(x):
    high = x.astype(BF16)
    return high, (x - high.astype(F32)).astype(BF16)


def mm3(a, b, kind=NN):
    ah, al = split(a)
    bh, bl = split(b)
    return dot(
        jnp.concatenate([ah, ah, al], axis=kind[0]),
        jnp.concatenate([bh, bl, bh], axis=kind[1]),
        kind,
    )


def mm2(a, b, kind=NN):
    bh, bl = split(b)
    return dot(
        jnp.concatenate([a, a], axis=kind[0]), jnp.concatenate([bh, bl], axis=kind[1]), kind
    )


def mm1(a, b, kind=NN):
    return dot(a.astype(BF16), b.astype(BF16), kind)


def one_hot(condition):
    return jnp.where(condition, 1.0, 0.0).astype(BF16)


def iota(shape, dim):
    return lax.broadcasted_iota(jnp.int32, shape, dim)


def clip_start(lengths, positions):
    begin = jnp.zeros_like(positions)
    end = jnp.int32(0)
    for c in range(lengths.shape[0]):
        size = lengths[c]
        end = end + size
        begin = begin + jnp.where(end <= positions, size, 0)
    return begin


def kernel(
    dims,
    loaded,
    out_grad,
    w_query,
    w_key,
    w_value,
    w_beta,
    beta_max,
    out_gain,
    clip_lengths,
    delay_offsets,
    block_order,
    both_out,
    wq,
    wk,
    wv,
    cot,
    r1,
    s2,
    r2,
    tails,
    feat,
    acc,
    ab,
    sib_ab,
    plane,
    group,
    from_z1,
    from_z2,
    a_next,
    states,
    grads,
    sib_grad,
    gplane,
    ggroup,
    gz1,
    gz2,
    dstates,
    gcat,
    rs_send,
    rs_recv,
    summed,
    follow,
    give_s,
    give_d,
    local_sem,
    send_sem,
    recv_sem,
):
    Z, X, H, F, W = dims["Z"], dims["X"], dims["H"], dims["F"], dims["W"]
    C = CORES
    G = X * C
    S = Z * G
    BR = F // S
    N = 128
    CB = delay_offsets.shape[0]
    seq, y = lax.axis_index("seq"), lax.axis_index("head")
    z = lax.div(seq, G)
    g = lax.rem(seq, G)
    x = lax.div(g, C)
    core = lax.rem(g, C)
    other = 1 - core

    def at(zz, gg):
        return (zz * G + gg, y)

    counter = [0]
    started = []

    def remote(src, dst, device, index=None):
        if index is None:
            index = counter[0]
            counter[0] += 1
        return pltpu.make_async_remote_copy(
            src_ref=src,
            dst_ref=dst,
            send_sem=send_sem.at[index],
            recv_sem=recv_sem.at[index],
            device_id=device,
            device_id_type=pl.DeviceIdType.MESH,
        )

    def go(copy):
        copy.start()
        started.append(copy)
        return copy

    fetches = [
        pltpu.make_async_copy(src, dst, local_sem.at[i])
        for i, (src, dst) in enumerate(
            ((w_query, wq), (w_key, wk), (w_value, wv), (out_grad, cot))
        )
    ]
    partners = [at(lax.rem(z + k, Z), g) for k in range(1, Z)]
    partners += [at(z, lax.rem(g + k, G)) for k in range(1, G)]
    partners += [(lax.rem(seq + 1, S), y), (lax.rem(seq + S - 1, S), y)]
    partners += [(seq, lax.rem(y + k, H)) for k in range(1, H)]
    barrier = pltpu.get_barrier_semaphore()
    for partner in partners:
        pl.semaphore_signal(barrier, inc=1, device_id=partner, device_id_type=pl.DeviceIdType.MESH)
    pl.semaphore_wait(barrier, len(partners))

    rows1 = G * BR
    copies = []
    for k in range(1, Z):
        to = lax.rem(z + k, Z)
        src = loaded.at[pl.ds(pl.multiple_of(to * rows1, rows1), rows1)]
        copies.append(go(remote(src, r1.at[z], at(to, g))))
    own_rows = loaded.at[pl.ds(pl.multiple_of(z * rows1, rows1), rows1)]
    keep = pltpu.make_async_copy(own_rows, r1.at[z], local_sem.at[4])
    keep.start()

    for copy in fetches:
        copy.start()

    first = seq * F
    pos_col = first + iota((F, 1), 0)
    begin_col = clip_start(clip_lengths, pos_col)
    begin_row = clip_start(clip_lengths, first + iota((1, F), 1))
    delay = delay_offsets[lax.div(y * CB, H)]
    row, col = iota((F, F), 0), iota((F, F), 1)
    same = jnp.where(begin_col == begin_row, 1.0, 0.0)
    low = jnp.where(row > col, same, 0.0)
    low_eq = jnp.where(row >= col, same, 0.0)
    eye = jnp.where(row == col, 1.0, 0.0)
    carried = jnp.where(begin_col < first, 1.0, 0.0)
    final = jnp.where(begin_col == begin_col[F - 1 : F, :], 1.0, 0.0)
    carried_last = carried[F - 1 : F, :]

    zbr = Z * BR
    to_g, to_z, to_r = row // zbr, (row % zbr) // BR, row % BR
    regroup = one_hot(col == to_z * rows1 + to_g * BR + to_r)
    order = jnp.broadcast_to(block_order[...], (16, S)).astype(F32).astype(BF16)
    src_i, out_q = iota((S, F), 0), iota((S, F), 1)
    spread = one_hot(src_i == ((out_q % zbr) // BR) * G + out_q // zbr)
    target = dot(order, spread)[0:1, :].astype(jnp.int32) * BR + iota((1, F), 1) % BR
    place = one_hot(row == target)

    for copy in copies:
        copy.wait_recv()
    keep.wait()
    s2[...] = dot(regroup, r1[...].reshape(F, W)).astype(BF16).reshape(G, zbr, W)
    copies = []
    for k in range(1, G):
        to = lax.rem(g + k, G)
        copies.append(go(remote(s2.at[to], r2.at[g], at(z, to))))
    r2[g] = s2[g]
    for copy in copies:
        copy.wait_recv()
    feat[y] = dot(place, r2[...].reshape(F, W)).astype(BF16)

    half = F // 2

    def ring(k):
        return lax.rem(y + k + H, H)

    def along(k):
        return (seq, ring(k))

    halo = go(remote(feat.at[y, pl.ds(F - 16, 16)], tails.at[y], (lax.rem(seq + 1, S), y)))
    direct = {}
    for ks in ((2, -2), (1, -1)):
        for b in range(2):
            own = feat.at[y, pl.ds(b * half, half)]
            for k in ks:
                direct[k, b] = go(remote(own, own, along(k)))
    halo.wait_recv()
    tail_sends = {k: go(remote(tails.at[y], tails.at[y], along(k))) for k in range(1, H)}

    def project(owner, begin):
        delay = delay_offsets[lax.div(owner * CB, H)]
        source = jnp.where(pos_col - delay >= begin_col, iota((F, 1), 0) - delay, -100)
        shift = one_hot(source == iota((F, F + 16), 1) - 16)
        block = dot(shift, jnp.concatenate([tails[owner], feat[owner]], axis=0)).astype(BF16)
        here = pl.ds(pl.multiple_of(owner * W, W), W)
        for i, weight in enumerate((wq, wk, wv)):
            value = dot(block, weight[here, :])
            at_cols = slice(i * W, (i + 1) * W)
            acc[:, at_cols] = value if begin else acc[:, at_cols] + value
        value = dot(block, w_beta[:, here], NT)
        acc[:, 3 * W : 3 * W + 2] = value if begin else acc[:, 3 * W : 3 * W + 2] + value

    for copy in fetches:
        copy.wait()
    project(y, True)
    relays = {}
    for b in range(2):
        for d in (1, -1):
            direct[2 * d, b].wait_recv()
            block = feat.at[ring(-2 * d), pl.ds(b * half, half)]
            relays[3 * d, b] = go(remote(block, block, along(d)))
            if b == (0 if d == 1 else 1):
                relays[4 * d, b] = go(remote(block, block, along(2 * d)))
    for k in (2, -2, 1, -1):
        if k in (1, -1):
            for b in range(2):
                direct[k, b].wait_recv()
        tail_sends[k % H].wait_recv()
        project(ring(-k), False)
    for k in (3, -3):
        for b in range(2):
            relays[k, b].wait_recv()
        tail_sends[k % H].wait_recv()
        project(ring(-k), False)
    relays[4, 0].wait_recv()
    relays[-4, 1].wait_recv()
    tail_sends[4].wait_recv()
    project(ring(4), False)

    heads = range(2)
    Q, K, V, beta, nq, nk, sig, Gm, T = ({} for _ in range(9))
    for h in heads:
        cols = slice(h * N, (h + 1) * N)
        q_raw, k_raw = acc[:, cols], acc[:, W + h * N : W + (h + 1) * N]
        V[h] = acc[:, 2 * W + h * N : 2 * W + (h + 1) * N]
        nq[h] = lax.rsqrt(jnp.sum(q_raw * q_raw, axis=1, keepdims=True) + EPSILON)
        nk[h] = lax.rsqrt(jnp.sum(k_raw * k_raw, axis=1, keepdims=True) + EPSILON)
        Q[h], K[h] = q_raw * nq[h], k_raw * nk[h]
        sig[h] = 1.0 / (1.0 + jnp.exp(-acc[:, 3 * W + h : 3 * W + h + 1]))
        beta[h] = beta_max[h] * sig[h]
    L = {}
    for h in heads:
        Gm[h] = mm3(K[h], K[h], NT) * low
        L[h] = beta[h] * Gm[h]
    size = 1
    while size < F:
        pair = (
            ((row // (2 * size)) == (col // (2 * size)))
            & ((row // size) % 2 == 1)
            & ((col // size) % 2 == 0)
        )
        inner = {h: jnp.where(pair, L[h], 0.0) for h in heads}
        if size == 1:
            T = {h: eye - inner[h] for h in heads}
        else:
            half_way = {h: mm3(T[h], inner[h]) for h in heads}
            T = {h: T[h] - mm3(half_way[h], T[h]) for h in heads}
        size *= 2
    Wk, Wv = {}, {}
    for h in heads:
        both = mm3(T[h], beta[h] * jnp.concatenate([K[h], V[h]], axis=1))
        Wk[h], Wv[h] = both[:, :N], both[:, N:]
    for h in heads:
        both = mm3(K[h], jnp.concatenate([Wk[h], final * Wv[h]], axis=1), TN)
        ab[h, :, :N] = carried_last * (eye - both[:, :N])
        ab[h, :, N:] = both[:, N:]

    sibling = at(z, x * C + other)
    copy = go(remote(ab.at[other], sib_ab, sibling))
    P_, Oloc, R = {}, {}, {}
    for h in heads:
        P_[h] = mm3(Q[h], K[h], NT) * low_eq
        both = mm3(P_[h], jnp.concatenate([carried * Wk[h], Wv[h]], axis=1))
        R[h] = carried * Q[h] - both[:, :N]
        Oloc[h] = both[:, N:]
    copy.wait_recv()
    own, sib = ab[core], sib_ab[...]
    early = jnp.where(core == 0, own, sib)
    late = jnp.where(core == 0, sib, own)
    a_early, b_early = early[:, :N], early[:, N:]
    a_late, b_late = late[:, :N], late[:, N:]
    zero = jnp.zeros((N, N), F32)
    pad_b = jnp.concatenate([zero, b_late], axis=1)
    plane[x] = (mm3(a_late, early) + pad_b).astype(BF16)
    copies = []
    for k in range(1, X):
        to = lax.rem(x + k, X)
        copies.append(go(remote(plane.at[x], plane.at[x], at(z, to * C + core))))
    for copy in copies:
        copy.wait_recv()

    def then(before, after):
        shift = jnp.concatenate([zero, after[:, N:].astype(F32)], axis=1)
        return mm2(after[:, :N], before) + shift

    def then32(before, after):
        shift = jnp.concatenate([zero, after[:, N:]], axis=1)
        return mm3(after[:, :N], before) + shift

    maps = [plane[i] for i in range(X)]
    identity = jnp.concatenate([eye, zero], axis=1)
    prefix = [identity, maps[0].astype(F32)]
    if X == 4:
        front = then(prefix[1], maps[1])
        back = then(maps[2].astype(F32), maps[3])
        total = then32(front, back)
        prefix += [front]
    else:
        for i in range(1, X):
            total = then(prefix[-1], maps[i])
            prefix.append(total)
    group[...] = total.astype(BF16)
    z1, z2 = lax.rem(z + 1, Z), lax.rem(z + 2, Z)
    y1, y2 = lax.rem(z + Z - 1, Z), lax.rem(z + Z - 2, Z)
    copies = [
        go(remote(group, from_z1, at(z1, g))),
        go(remote(group.at[:, pl.ds(N, N)], from_z2, at(z2, g))),
    ]
    next_copy = go(remote(group.at[:, pl.ds(0, N)], a_next, at(y1, g)))
    if X == 4:
        prefix.append(then(front, maps[2]))
        a1, a2, a3 = (maps[i][:, :N] for i in (1, 2, 3))
        suffix = [mm2(a3, mm2(a2, a1.astype(F32))), back[:, :N], a3.astype(F32), eye]
    else:
        suffix = [eye]
        for i in range(X - 1, 0, -1):
            suffix.insert(0, mm3(suffix[0], maps[i][:, :N].astype(F32)))

    def pick(options, index):
        value = options[0]
        for i in range(1, len(options)):
            value = jnp.where(index == i, options[i], value)
        return value

    before_me = pick(prefix[:X], x)
    after_me = pick(suffix, x)
    for copy in copies:
        copy.wait_recv()
    s_group = from_z1[:, N:].astype(F32) + dot(from_z1[:, :N], from_z2[...])
    s_chip = before_me[:, N:] + mm3(before_me[:, :N], s_group)
    s_late = b_early + mm3(a_early, s_chip)
    states[core] = jnp.where(core == 0, s_chip, s_late)
    give_s[...] = jnp.where(core == 0, s_late, s_chip)
    go(remote(give_s, states.at[core], sibling)).wait_recv()

    gain = out_gain[...]
    O, dO = {}, {}
    for h in heads:
        cols = slice(h * N, (h + 1) * N)
        O[h] = Oloc[h] + mm3(R[h], states[h])
        inv = lax.rsqrt(jnp.mean(O[h] * O[h], axis=1, keepdims=True) + EPSILON)
        both_out[0, :, cols] = (O[h] * inv * gain).astype(BF16)
        scaled = cot[:, cols].astype(F32) * gain
        unit = O[h] * inv
        dO[h] = inv * (scaled - unit * jnp.mean(scaled * unit, axis=1, keepdims=True))
        grads[h] = mm3(R[h], dO[h], TN)
    copy = go(remote(grads.at[other], sib_grad, sibling))
    U, dU0, Y, dX0, dP, dQ, dK0, Zv = ({} for _ in range(8))
    for h in heads:
        S0 = states[h]
        KS = carried * mm3(K[h], S0)
        Zv[h] = V[h] - KS
        U[h] = Wv[h] - carried * mm3(Wk[h], S0)
    copy.wait_recv()
    own, sib = grads[core], sib_grad[...]
    g_early = jnp.where(core == 0, own, sib)
    g_late = jnp.where(core == 0, sib, own)
    gplane[x] = (g_early + mm3(a_early, g_late, TN)).astype(BF16)
    copies = []
    for k in range(1, X):
        to = lax.rem(x + k, X)
        copies.append(go(remote(gplane.at[x], gplane.at[x], at(z, to * C + core))))
    for h in heads:
        dU0[h] = mm3(P_[h], dO[h], TN)
        both = mm3(T[h], jnp.concatenate([dU0[h], final * K[h]], axis=1), TN)
        dX0[h], Y[h] = both[:, :N], both[:, N:]
    for copy in copies:
        copy.wait_recv()
    gs = [gplane[i].astype(F32) for i in range(X)]

    def back_through(i, later):
        return gs[i] + mm2(maps[i][:, :N], later, TN)

    if X == 4:
        pair_late = back_through(2, gs[3])
        pair_early = back_through(0, gs[1])
        g_total = pair_early + mm3(front[:, :N], pair_late, TN)
        behind = [back_through(1, pair_late), pair_late, gs[3], zero]
    else:
        behind = [zero]
        for i in range(X - 1, -1, -1):
            behind.insert(0, back_through(i, behind[0]))
        g_total = behind[0]
        behind = behind[1:]
    ggroup[...] = g_total.astype(BF16)
    copies = [
        go(remote(ggroup, gz1, at(y1, g))),
        go(remote(ggroup, gz2, at(y2, g))),
    ]
    behind_me = pick(behind, x)
    for h in heads:
        S0 = states[h]
        dP[h] = mm3(dO[h], U[h], NT) * low_eq
        dQ[h] = carried * mm3(dO[h], S0, NT) + mm3(dP[h], K[h])
        dK0[h] = mm3(dP[h], Q[h], TN)
        grad = nq[h] * (dQ[h] - Q[h] * jnp.sum(Q[h] * dQ[h], axis=1, keepdims=True))
        gcat[:, h * N : (h + 1) * N] = grad.astype(BF16)
    next_copy.wait_recv()
    for copy in copies:
        copy.wait_recv()
    d_group = gz1[...].astype(F32) + dot(a_next[...], gz2[...], TN)
    d_chip = behind_me + mm3(after_me, d_group, TN)
    d_early = g_late + mm3(a_late, d_chip, TN)
    dstates[core] = jnp.where(core == 0, d_early, d_chip)
    give_d[...] = jnp.where(core == 0, d_chip, d_early)
    go(remote(give_d, dstates.at[core], sibling)).wait_recv()

    dlog = {}
    for h in heads:
        S0, dS = states[h], dstates[h]
        dX = dX0[h] + mm3(Y[h], dS)
        scaled = beta[h] * dX
        both = mm3(dX, jnp.concatenate([U[h], S0], axis=0), NT)
        dL = -both[:, :F] * low
        dG = beta[h] * dL
        dK = dK0[h] + mm3(final * U[h], dS, NT)
        dK = dK - carried * beta[h] * both[:, F:]
        dK = dK + mm3(dG, K[h]) + mm3(dG, K[h], TN)
        d_beta = jnp.sum(dX * Zv[h], axis=1, keepdims=True)
        d_beta = d_beta + jnp.sum(dL * Gm[h], axis=1, keepdims=True)
        grad = nk[h] * (dK - K[h] * jnp.sum(K[h] * dK, axis=1, keepdims=True))
        gcat[:, W + h * N : W + (h + 1) * N] = grad.astype(BF16)
        gcat[:, 2 * W + h * N : 2 * W + (h + 1) * N] = scaled.astype(BF16)
        d_logit = d_beta * beta[h] * (1.0 - sig[h])
        dlog[h] = d_logit.astype(BF16).astype(F32)

    def partial(owner):
        here = pl.ds(pl.multiple_of(owner * W, W), W)
        rows = w_beta[:, here].astype(F32)
        value = dlog[0] * rows[0:1, :] + dlog[1] * rows[1:2, :]
        for i, weight in enumerate((wq, wk, wv)):
            value = value + dot(gcat[:, i * W : (i + 1) * W], weight[here, :], NT)
        return value

    hop = (-1, 1, -2, 2, -1, 1, -2, 2)
    parts = {}

    chunks = ((0, 16), (16, half), (half, F))

    def send_rows(kind, b, value):
        rows = pl.ds(chunks[b][0], chunks[b][1] - chunks[b][0])
        src, dst = rs_send.at[kind, rows], rs_recv.at[kind, rows]
        if kind in (2, 3):
            src, dst = src.at[:, pl.ds(0, N)], dst.at[:, pl.ds(0, N)]
            rs_send[kind, rows, :N] = value.astype(BF16)
        else:
            rs_send[kind, rows] = value.astype(BF16)
        reduces[kind, b] = go(remote(src, dst, along(hop[kind])))

    def rows_of(k, b):
        return parts[k][chunks[b][0] : chunks[b][1], :]

    def received(kind, b):
        reduces[kind, b].wait_recv()
        return rs_recv[kind, chunks[b][0] : chunks[b][1], :]

    reduces = {}
    for k in (-3, 3, 4):
        parts[k] = partial(ring(k))
    for b in range(3):
        send_rows(0, b, rows_of(-3, b))
        send_rows(1, b, rows_of(3, b))
        send_rows(2, b, rows_of(4, b)[:, :N])
        send_rows(3, b, rows_of(4, b)[:, N:])
    for k in (-1, 1):
        parts[k] = partial(ring(k))
    for b in range(3):
        send_rows(4, b, rows_of(-1, b))
        send_rows(5, b, rows_of(1, b))
    for k in (-2, 2, 0):
        parts[k] = partial(ring(k))

    def hand_on(b):
        for kind, k in ((6, -2), (7, 2)):
            value = rows_of(k, b) + received(kind - 6, b).astype(F32)
            extra = received(kind - 4, b)[:, :N].astype(F32)
            blank = jnp.zeros_like(extra)
            extra = jnp.concatenate([extra, blank] if kind == 6 else [blank, extra], axis=1)
            send_rows(kind, b, value + extra)

    def finish_rows(b):
        value = rows_of(0, b)
        for kind in (4, 5, 6, 7):
            value = value + received(kind, b).astype(F32)
        summed[chunks[b][0] : chunks[b][1], :] = value.astype(BF16)

    for b in range(3):
        hand_on(b)
    for b in range(3):
        finish_rows(b)
        if b == 0:
            halo = go(remote(summed.at[pl.ds(0, 16)], follow, (lax.rem(seq + S - 1, S), y)))
    ahead = pos_col + delay
    reaches = (ahead < S * F) & (clip_start(clip_lengths, ahead) <= pos_col)
    wanted = jnp.where(reaches, ahead - first, -1)
    pull = one_hot(wanted == iota((F, F + 16), 1))
    halo.wait_recv()
    both = jnp.concatenate([summed[...], follow[...]], axis=0)
    both_out[1] = dot(pull, both).astype(BF16)
    for copy in started:
        copy.wait_send()


def on_device(
    dims,
    loaded,
    out_grad,
    w_query,
    w_key,
    w_value,
    w_beta,
    beta_max,
    out_gain,
    clip_lengths,
    delay_offsets,
    block_order,
):
    Z, X, H = dims["Z"], dims["X"], dims["H"]
    F, W = dims["F"], dims["W"]
    G = X * CORES
    BR = F // (Z * G)
    N = 128
    count = 128
    vmem, smem, anyw = (
        pl.BlockSpec(memory_space=s) for s in (pltpu.VMEM, pltpu.SMEM, pl.ANY)
    )
    D = w_query.shape[0]
    scratch = [
        pltpu.VMEM((D, W), BF16),
        pltpu.VMEM((D, W), BF16),
        pltpu.VMEM((D, W), BF16),
        pltpu.VMEM((F, W), BF16),
        pltpu.VMEM((Z, G * BR, W), BF16),
        pltpu.VMEM((G, Z * BR, W), BF16),
        pltpu.VMEM((G, Z * BR, W), BF16),
        pltpu.VMEM((H, 16, W), BF16),
        pltpu.VMEM((H, F, W), BF16),
        pltpu.VMEM((F, 3 * W + 128), F32),
        pltpu.VMEM((2, N, 2 * N), F32),
        pltpu.VMEM((N, 2 * N), F32),
        pltpu.VMEM((X, N, 2 * N), BF16),
        pltpu.VMEM((N, 2 * N), BF16),
        pltpu.VMEM((N, 2 * N), BF16),
        pltpu.VMEM((N, N), BF16),
        pltpu.VMEM((N, N), BF16),
        pltpu.VMEM((2, N, N), F32),
        pltpu.VMEM((2, N, N), F32),
        pltpu.VMEM((N, N), F32),
        pltpu.VMEM((X, N, N), BF16),
        pltpu.VMEM((N, N), BF16),
        pltpu.VMEM((N, N), BF16),
        pltpu.VMEM((N, N), BF16),
        pltpu.VMEM((2, N, N), F32),
        pltpu.VMEM((F, 3 * W), BF16),
        pltpu.VMEM((8, F, W), BF16),
        pltpu.VMEM((8, F, W), BF16),
        pltpu.VMEM((F, W), BF16),
        pltpu.VMEM((16, W), BF16),
        pltpu.VMEM((N, N), F32),
        pltpu.VMEM((N, N), F32),
        pltpu.SemaphoreType.DMA((5,)),
        pltpu.SemaphoreType.DMA((count,)),
        pltpu.SemaphoreType.DMA((count,)),
    ]
    result = pl.pallas_call(
        functools.partial(kernel, dims),
        out_shape=jax.ShapeDtypeStruct((2, F, W), BF16),
        in_specs=[anyw, anyw, anyw, anyw, anyw, vmem, smem, vmem, smem, smem, vmem],
        out_specs=vmem,
        scratch_shapes=scratch,
        compiler_params=pltpu.CompilerParams(
            collective_id=0, has_side_effects=True, vmem_limit_bytes=60 * 2**20
        ),
    )(
        loaded,
        out_grad,
        w_query,
        w_key,
        w_value,
        w_beta.T,
        beta_max,
        out_gain.reshape(1, -1),
        clip_lengths,
        delay_offsets,
        block_order,
    )
    return result[0], result[1]


def build(mesh, chips_x, frames):
    seq, head = mesh.shape["seq"], mesh.shape["head"]
    dims = dict(Z=seq // (chips_x * CORES), X=chips_x, H=head, F=frames, W=256)
    return jax.shard_map(
        functools.partial(on_device, dims),
        mesh=mesh,
        in_specs=(
            P("seq", "head"),
            P("seq", "head"),
            P(None, "head"),
            P(None, "head"),
            P(None, "head"),
            P(None, "head"),
            P("head"),
            P(),
            P(),
            P(),
            P("seq", None),
        ),
        out_specs=(P("seq", "head"), P("seq", "head")),
        check_vma=False,
    )


def solution(mesh):
    return build(mesh, CHIPS_X, 128)
```

```python
import functools

import jax
import jax.numpy as jnp
from jax import lax
from jax.experimental import pallas as pl
from jax.experimental.pallas import tpu as pltpu
from jax.sharding import PartitionSpec as P

EPSILON = 1e-06
F32, BF16 = jnp.float32, jnp.bfloat16
CORES = 2
CHIPS_X = 4

NN = (1, 0)
NT = (1, 1)
TN = (0, 0)


def dot(a, b, kind=NN):
    return lax.dot_general(
        a, b, (((kind[0],), (kind[1],)), ((), ())), preferred_element_type=F32
    )


def split(x):
    high = x.astype(BF16)
    return high, (x - high.astype(F32)).astype(BF16)


def mm3(a, b, kind=NN):
    ah, al = split(a)
    bh, bl = split(b)
    return dot(
        jnp.concatenate([ah, ah, al], axis=kind[0]),
        jnp.concatenate([bh, bl, bh], axis=kind[1]),
        kind,
    )


def mm2(a, b, kind=NN):
    bh, bl = split(b)
    return dot(
        jnp.concatenate([a, a], axis=kind[0]), jnp.concatenate([bh, bl], axis=kind[1]), kind
    )


def mm1(a, b, kind=NN):
    return dot(a.astype(BF16), b.astype(BF16), kind)


def one_hot(condition):
    return jnp.where(condition, 1.0, 0.0).astype(BF16)


def iota(shape, dim):
    return lax.broadcasted_iota(jnp.int32, shape, dim)


def clip_start(lengths, positions):
    begin = jnp.zeros_like(positions)
    end = jnp.int32(0)
    for c in range(lengths.shape[0]):
        size = lengths[c]
        end = end + size
        begin = begin + jnp.where(end <= positions, size, 0)
    return begin


def kernel(
    dims,
    loaded,
    out_grad,
    w_query,
    w_key,
    w_value,
    w_beta,
    beta_max,
    out_gain,
    clip_lengths,
    delay_offsets,
    block_order,
    both_out,
    wq,
    wk,
    wv,
    cot,
    s1,
    r1,
    s2,
    r2,
    last,
    tail,
    feat,
    acc,
    raw,
    pair_raw,
    plane,
    group,
    from_z1,
    from_z2,
    a_next,
    out_pair,
    out_heads,
    gplane,
    ggroup,
    gz1,
    gz2,
    grad_pair,
    grad_heads,
    rs_send,
    rs_recv,
    summed,
    follow,
    local_sem,
    send_sem,
    recv_sem,
):
    Z, X, H, F, W = dims["Z"], dims["X"], dims["H"], dims["F"], dims["W"]
    C = CORES
    G = X * C
    S = Z * G
    BR = F // S
    N = 128
    CB = delay_offsets.shape[0]
    seq, y = lax.axis_index("seq"), lax.axis_index("head")
    z = lax.div(seq, G)
    g = lax.rem(seq, G)
    x = lax.div(g, C)
    core = lax.rem(g, C)
    other = 1 - core

    def at(zz, gg):
        return (zz * G + gg, y)

    counter = [0]
    started = []

    def remote(src, dst, device, index=None):
        if index is None:
            index = counter[0]
            counter[0] += 1
        return pltpu.make_async_remote_copy(
            src_ref=src,
            dst_ref=dst,
            send_sem=send_sem.at[index],
            recv_sem=recv_sem.at[index],
            device_id=device,
            device_id_type=pl.DeviceIdType.MESH,
        )

    def go(copy):
        copy.start()
        started.append(copy)
        return copy

    fetches = [
        pltpu.make_async_copy(src, dst, local_sem.at[i])
        for i, (src, dst) in enumerate(
            ((w_query, wq), (w_key, wk), (w_value, wv))
        )
    ]
    partners = [at(lax.rem(z + k, Z), g) for k in range(1, Z)]
    partners += [at(z, lax.rem(g + k, G)) for k in range(1, G)]
    partners += [(lax.rem(seq + 1, S), y), (lax.rem(seq + S - 1, S), y)]
    partners += [(seq, lax.rem(y + k, H)) for k in range(1, H)]
    barrier = pltpu.get_barrier_semaphore()
    for partner in partners:
        pl.semaphore_signal(barrier, inc=1, device_id=partner, device_id_type=pl.DeviceIdType.MESH)

    rows1, zbr = G * BR, Z * BR
    row, col = iota((F, F), 0), iota((F, F), 1)
    to_g, to_z = row // zbr, (row % zbr) // BR
    regroup = one_hot(col == to_z * rows1 + to_g * BR + row % BR)
    s1[...] = dot(regroup, loaded[...]).astype(BF16).reshape(G, zbr, W)
    pl.semaphore_wait(barrier, len(partners))
    copies = []
    for k in range(1, G):
        to = lax.rem(g + k, G)
        copies.append(go(remote(s1.at[to], r1.at[g], at(z, to))))
    r1[g] = s1[g]
    sibling = at(z, x * C + other)

    def head_columns(h):
        return out_grad.at[:, pl.ds(pl.multiple_of(h * N, N), N)]

    cot_copy = go(remote(head_columns(other), cot.at[core], sibling))
    cot_keep = pltpu.make_async_copy(head_columns(core), cot.at[core], local_sem.at[3])
    cot_keep.start()
    for copy in fetches:
        copy.start()

    first = seq * F
    pos_col = first + iota((F, 1), 0)
    begin_col = clip_start(clip_lengths, pos_col)
    delay = delay_offsets[lax.div(y * CB, H)]
    eye = jnp.where(row == col, 1.0, 0.0)
    low, low_eq, carried, final, carried_last = ([] for _ in range(5))
    for i in range(C):
        start = (seq - core + i) * F
        at_col = clip_start(clip_lengths, start + iota((F, 1), 0))
        at_row = clip_start(clip_lengths, start + iota((1, F), 1))
        same = jnp.where(at_col == at_row, 1.0, 0.0)
        low.append(jnp.where(row > col, same, 0.0))
        low_eq.append(jnp.where(row >= col, same, 0.0))
        carried.append(jnp.where(at_col < start, 1.0, 0.0))
        final.append(jnp.where(at_col == at_col[F - 1 : F, :], 1.0, 0.0))
        carried_last.append(carried[i][F - 1 : F, :])

    order = jnp.broadcast_to(block_order[...], (16, S)).astype(F32).astype(BF16)
    spread = one_hot(iota((S, F), 0) == iota((S, F), 1) // BR)
    target = dot(order, spread)[0:1, :].astype(jnp.int32) * BR + iota((1, F), 1) % BR
    place = one_hot(row == target)
    to_g, to_z = (row % rows1) // BR, row // rows1
    back_to_z = one_hot(col == to_g * zbr + to_z * BR + row % BR)

    for copy in copies:
        copy.wait_recv()
    s2[...] = dot(back_to_z, r1[...].reshape(F, W)).astype(BF16).reshape(Z, rows1, W)
    copies = []
    for k in range(1, Z):
        to = lax.rem(z + k, Z)
        copies.append(go(remote(s2.at[to], r2.at[z], at(to, g))))
    r2[z] = s2[z]
    for copy in copies:
        copy.wait_recv()
    arranged = dot(place, r2[...].reshape(F, W)).astype(BF16)
    last[...] = arranged[F - 16 :, :]

    half = F // 2
    chunks = ((half, F), (16, half), (0, 16))

    def ring(k):
        return lax.rem(y + k + H, H)

    def along(k):
        return (seq, ring(k))

    halo = go(remote(last, tail, (lax.rem(seq + 1, S), y)))
    source = jnp.where(pos_col - delay >= begin_col, iota((F, 1), 0) - delay, -100)
    direct = {}

    def send_own(b):
        own = feat.at[y, pl.ds(chunks[b][0], chunks[b][1] - chunks[b][0])]
        for k in (2, -2, 1, -1):
            direct[k, b] = go(remote(own, own, along(k)))

    shift = one_hot(source == iota((F, F), 1))
    feat[y, half:, :] = dot(shift[half:, :], arranged).astype(BF16)
    send_own(0)
    early = dot(shift[:half, :], arranged)
    feat[y, 16:half, :] = early[16:, :].astype(BF16)
    send_own(1)
    halo.wait_recv()
    shift = one_hot(source[:16, :] == iota((16, 16), 1) - 16)
    feat[y, 0:16, :] = (early[:16, :] + dot(shift, tail[...])).astype(BF16)
    send_own(2)

    def project(owner, begin):
        block = feat[owner]
        here = pl.ds(pl.multiple_of(owner * W, W), W)
        for i, weight in enumerate((wq, wk, wv)):
            value = dot(block, weight[here, :])
            at_cols = slice(i * W, (i + 1) * W)
            acc[:, at_cols] = value if begin else acc[:, at_cols] + value
        value = dot(block, w_beta[:, here], NT)
        acc[:, 3 * W : 3 * W + 2] = value if begin else acc[:, 3 * W : 3 * W + 2] + value

    for copy in fetches:
        copy.wait()
    project(y, True)
    relays = {}
    for b in range(3):
        for d in (1, -1):
            direct[2 * d, b].wait_recv()
            block = feat.at[ring(-2 * d), pl.ds(chunks[b][0], chunks[b][1] - chunks[b][0])]
            relays[3 * d, b] = go(remote(block, block, along(d)))
            if (b == 0) == (d == 1):
                relays[4 * d, b] = go(remote(block, block, along(2 * d)))
    for k in (2, -2, 1, -1):
        if k in (1, -1):
            for b in range(3):
                direct[k, b].wait_recv()
        project(ring(-k), False)
    for k in (3, -3):
        for b in range(3):
            relays[k, b].wait_recv()
        project(ring(-k), False)
    for k, b in ((4, 0), (-4, 1), (-4, 2)):
        relays[k, b].wait_recv()
    project(ring(4), False)

    for h in range(C):
        for i in range(3):
            raw[h, :, i * N : (i + 1) * N] = acc[:, i * W + h * N : i * W + (h + 1) * N]
        raw[h, :, 3 * N :] = jnp.broadcast_to(acc[:, 3 * W + h : 3 * W + h + 1], (F, N))
    copy = go(remote(raw.at[other], pair_raw.at[core], sibling))
    pair_raw[core] = raw[core]
    copy.wait_recv()

    both_cores = range(C)
    Q, K, V, beta, nq, nk, sig, Gm, T = ({} for _ in range(9))
    for h in both_cores:
        q_raw, k_raw = pair_raw[h, :, :N], pair_raw[h, :, N : 2 * N]
        V[h] = pair_raw[h, :, 2 * N : 3 * N]
        nq[h] = lax.rsqrt(jnp.sum(q_raw * q_raw, axis=1, keepdims=True) + EPSILON)
        nk[h] = lax.rsqrt(jnp.sum(k_raw * k_raw, axis=1, keepdims=True) + EPSILON)
        Q[h], K[h] = q_raw * nq[h], k_raw * nk[h]
        sig[h] = 1.0 / (1.0 + jnp.exp(-pair_raw[h, :, 3 * N : 3 * N + 1]))
        beta[h] = beta_max[core] * sig[h]
    L = {}
    for h in both_cores:
        Gm[h] = mm3(K[h], K[h], NT) * low[h]
        L[h] = beta[h] * Gm[h]
    size = 1
    while size < F:
        pair = (
            ((row // (2 * size)) == (col // (2 * size)))
            & ((row // size) % 2 == 1)
            & ((col // size) % 2 == 0)
        )
        inner = {h: jnp.where(pair, L[h], 0.0) for h in both_cores}
        if size == 1:
            T = {h: eye - inner[h] for h in both_cores}
        else:
            half_way = {h: mm3(T[h], inner[h]) for h in both_cores}
            T = {h: T[h] - mm3(half_way[h], T[h]) for h in both_cores}
        size *= 2
    Wk, Wv, A, B = {}, {}, {}, {}
    for h in both_cores:
        both = mm3(T[h], beta[h] * jnp.concatenate([K[h], V[h]], axis=1))
        Wk[h], Wv[h] = both[:, :N], both[:, N:]
    for h in both_cores:
        both = mm3(K[h], jnp.concatenate([Wk[h], final[h] * Wv[h]], axis=1), TN)
        A[h] = carried_last[h] * (eye - both[:, :N])
        B[h] = both[:, N:]

    zero = jnp.zeros((N, N), F32)
    pad_b = jnp.concatenate([zero, B[1]], axis=1)
    plane[x] = (mm3(A[1], jnp.concatenate([A[0], B[0]], axis=1)) + pad_b).astype(BF16)
    copies = []
    for k in range(1, X):
        to = lax.rem(x + k, X)
        copies.append(go(remote(plane.at[x], plane.at[x], at(z, to * C + core))))
    P_, Oloc, R = {}, {}, {}
    for h in both_cores:
        P_[h] = mm3(Q[h], K[h], NT) * low_eq[h]
        both = mm3(P_[h], jnp.concatenate([carried[h] * Wk[h], Wv[h]], axis=1))
        R[h] = carried[h] * Q[h] - both[:, :N]
        Oloc[h] = both[:, N:]
    for copy in copies:
        copy.wait_recv()

    def then(before, after):
        shift = jnp.concatenate([zero, after[:, N:].astype(F32)], axis=1)
        return mm2(after[:, :N], before) + shift

    def then32(before, after):
        shift = jnp.concatenate([zero, after[:, N:]], axis=1)
        return mm3(after[:, :N], before) + shift

    maps = [plane[i] for i in range(X)]
    identity = jnp.concatenate([eye, zero], axis=1)
    prefix = [identity, maps[0].astype(F32)]
    if X == 4:
        front = then(prefix[1], maps[1])
        back = then(maps[2].astype(F32), maps[3])
        total = then32(front, back)
        prefix += [front]
    else:
        for i in range(1, X):
            total = then(prefix[-1], maps[i])
            prefix.append(total)
    group[...] = total.astype(BF16)
    z1, z2 = lax.rem(z + 1, Z), lax.rem(z + 2, Z)
    y1, y2 = lax.rem(z + Z - 1, Z), lax.rem(z + Z - 2, Z)
    copies = [
        go(remote(group, from_z1, at(z1, g))),
        go(remote(group.at[:, pl.ds(N, N)], from_z2, at(z2, g))),
    ]
    next_copy = go(remote(group.at[:, pl.ds(0, N)], a_next, at(y1, g)))
    if X == 4:
        prefix.append(then(front, maps[2]))
        a1, a2, a3 = (maps[i][:, :N] for i in (1, 2, 3))
        suffix = [mm2(a3, mm2(a2, a1.astype(F32))), back[:, :N], a3.astype(F32), eye]
    else:
        suffix = [eye]
        for i in range(X - 1, 0, -1):
            suffix.insert(0, mm3(suffix[0], maps[i][:, :N].astype(F32)))

    def pick(options, index):
        value = options[0]
        for i in range(1, len(options)):
            value = jnp.where(index == i, options[i], value)
        return value

    before_me = pick(prefix[:X], x)
    after_me = pick(suffix, x)
    for copy in copies:
        copy.wait_recv()
    s_group = from_z1[:, N:].astype(F32) + dot(from_z1[:, :N], from_z2[...])
    s_chip = before_me[:, N:] + mm3(before_me[:, :N], s_group)
    state = (s_chip, B[0] + mm3(A[0], s_chip))

    gain = out_gain[...]
    O, dO, ask = {}, {}, {}
    cot_copy.wait_recv()
    cot_keep.wait()
    for h in both_cores:
        O[h] = Oloc[h] + mm3(R[h], state[h])
        inv = lax.rsqrt(jnp.mean(O[h] * O[h], axis=1, keepdims=True) + EPSILON)
        out_pair[h] = (O[h] * inv * gain).astype(BF16)
        scaled = cot[h].astype(F32) * gain
        unit = O[h] * inv
        dO[h] = inv * (scaled - unit * jnp.mean(scaled * unit, axis=1, keepdims=True))
        ask[h] = mm3(R[h], dO[h], TN)
    gplane[x] = (ask[0] + mm3(A[0], ask[1], TN)).astype(BF16)
    copies = []
    for k in range(1, X):
        to = lax.rem(x + k, X)
        copies.append(go(remote(gplane.at[x], gplane.at[x], at(z, to * C + core))))
    out_copy = go(remote(out_pair.at[other], out_heads.at[core], sibling))
    out_heads[core] = out_pair[core]
    U, dU0, Y, dX0, dP, dQ, dK0, Zv = ({} for _ in range(8))
    for h in both_cores:
        Zv[h] = V[h] - carried[h] * mm3(K[h], state[h])
        U[h] = Wv[h] - carried[h] * mm3(Wk[h], state[h])
        dU0[h] = mm3(P_[h], dO[h], TN)
        both = mm3(T[h], jnp.concatenate([dU0[h], final[h] * K[h]], axis=1), TN)
        dX0[h], Y[h] = both[:, :N], both[:, N:]
    for copy in copies:
        copy.wait_recv()
    gs = [gplane[i].astype(F32) for i in range(X)]

    def back_through(i, later):
        return gs[i] + mm2(maps[i][:, :N], later, TN)

    if X == 4:
        pair_late = back_through(2, gs[3])
        pair_early = back_through(0, gs[1])
        g_total = pair_early + mm3(front[:, :N], pair_late, TN)
        behind = [back_through(1, pair_late), pair_late, gs[3], zero]
    else:
        behind = [zero]
        for i in range(X - 1, -1, -1):
            behind.insert(0, back_through(i, behind[0]))
        g_total = behind[0]
        behind = behind[1:]
    ggroup[...] = g_total.astype(BF16)
    copies = [
        go(remote(ggroup, gz1, at(y1, g))),
        go(remote(ggroup, gz2, at(y2, g))),
    ]
    behind_me = pick(behind, x)
    for h in both_cores:
        dP[h] = mm3(dO[h], U[h], NT) * low_eq[h]
        dQ[h] = carried[h] * mm3(dO[h], state[h], NT) + mm3(dP[h], K[h])
        dK0[h] = mm3(dP[h], Q[h], TN)
        grad = nq[h] * (dQ[h] - Q[h] * jnp.sum(Q[h] * dQ[h], axis=1, keepdims=True))
        grad_pair[h, :, :N] = grad.astype(BF16)
    next_copy.wait_recv()
    for copy in copies:
        copy.wait_recv()
    d_group = gz1[...].astype(F32) + dot(a_next[...], gz2[...], TN)
    d_chip = behind_me + mm3(after_me, d_group, TN)
    d_state = (ask[1] + mm3(A[1], d_chip, TN), d_chip)

    for h in both_cores:
        dX = dX0[h] + mm3(Y[h], d_state[h])
        both = mm3(dX, jnp.concatenate([U[h], state[h]], axis=0), NT)
        dL = -both[:, :F] * low[h]
        dG = beta[h] * dL
        dK = dK0[h] + mm3(final[h] * U[h], d_state[h], NT)
        dK = dK - carried[h] * beta[h] * both[:, F:]
        dK = dK + mm3(dG, K[h]) + mm3(dG, K[h], TN)
        d_beta = jnp.sum(dX * Zv[h], axis=1, keepdims=True)
        d_beta = d_beta + jnp.sum(dL * Gm[h], axis=1, keepdims=True)
        grad = nk[h] * (dK - K[h] * jnp.sum(K[h] * dK, axis=1, keepdims=True))
        d_logit = d_beta * beta[h] * (1.0 - sig[h])
        grad_pair[h, :, N : 2 * N] = grad.astype(BF16)
        grad_pair[h, :, 2 * N : 3 * N] = (beta[h] * dX).astype(BF16)
        grad_pair[h, :, 3 * N :] = jnp.broadcast_to(d_logit, (F, N)).astype(BF16)
    copy = go(remote(grad_pair.at[other], grad_heads.at[core], sibling))
    grad_heads[core] = grad_pair[core]
    copy.wait_recv()
    wide = [
        jnp.concatenate([grad_heads[h, :, i * N : (i + 1) * N] for h in range(C)], axis=1)
        for i in range(3)
    ]
    dlog = [grad_heads[h, :, 3 * N : 3 * N + 1].astype(F32) for h in range(C)]

    def partial(owner):
        here = pl.ds(pl.multiple_of(owner * W, W), W)
        rows = w_beta[:, here].astype(F32)
        value = dlog[0] * rows[0:1, :] + dlog[1] * rows[1:2, :]
        for i, weight in enumerate((wq, wk, wv)):
            value = value + dot(wide[i], weight[here, :], NT)
        return value

    hop = (-1, 1, -2, 2, -1, 1, -2, 2)
    parts = {}

    chunks = ((0, 16), (16, half), (half, F))

    def send_rows(kind, b, value):
        rows = pl.ds(chunks[b][0], chunks[b][1] - chunks[b][0])
        src, dst = rs_send.at[kind, rows], rs_recv.at[kind, rows]
        if kind in (2, 3):
            src, dst = src.at[:, pl.ds(0, N)], dst.at[:, pl.ds(0, N)]
            rs_send[kind, rows, :N] = value.astype(BF16)
        else:
            rs_send[kind, rows] = value.astype(BF16)
        reduces[kind, b] = go(remote(src, dst, along(hop[kind])))

    def rows_of(k, b):
        return parts[k][chunks[b][0] : chunks[b][1], :]

    def received(kind, b):
        reduces[kind, b].wait_recv()
        return rs_recv[kind, chunks[b][0] : chunks[b][1], :]

    reduces = {}
    for k in (-3, 3, 4):
        parts[k] = partial(ring(k))
    for b in range(3):
        send_rows(0, b, rows_of(-3, b))
        send_rows(1, b, rows_of(3, b))
        send_rows(2, b, rows_of(4, b)[:, :N])
        send_rows(3, b, rows_of(4, b)[:, N:])
    for k in (-1, 1):
        parts[k] = partial(ring(k))
    for b in range(3):
        send_rows(4, b, rows_of(-1, b))
        send_rows(5, b, rows_of(1, b))
    for k in (-2, 2, 0):
        parts[k] = partial(ring(k))

    def hand_on(b):
        for kind, k in ((6, -2), (7, 2)):
            value = rows_of(k, b) + received(kind - 6, b).astype(F32)
            extra = received(kind - 4, b)[:, :N].astype(F32)
            blank = jnp.zeros_like(extra)
            extra = jnp.concatenate([extra, blank] if kind == 6 else [blank, extra], axis=1)
            send_rows(kind, b, value + extra)

    def finish_rows(b):
        value = rows_of(0, b)
        for kind in (4, 5, 6, 7):
            value = value + received(kind, b).astype(F32)
        summed[chunks[b][0] : chunks[b][1], :] = value.astype(BF16)

    for b in range(3):
        hand_on(b)
    for b in range(3):
        finish_rows(b)
        if b == 0:
            halo = go(remote(summed.at[pl.ds(0, 16)], follow, (lax.rem(seq + S - 1, S), y)))
    ahead = pos_col + delay
    reaches = (ahead < S * F) & (clip_start(clip_lengths, ahead) <= pos_col)
    wanted = jnp.where(reaches, ahead - first, -1)
    pull = one_hot(wanted == iota((F, F + 16), 1))
    halo.wait_recv()
    both = jnp.concatenate([summed[...], follow[...]], axis=0)
    both_out[1] = dot(pull, both).astype(BF16)
    out_copy.wait_recv()
    for h in range(C):
        both_out[0, :, h * N : (h + 1) * N] = out_heads[h]
    for copy in started:
        copy.wait_send()


def on_device(
    dims,
    loaded,
    out_grad,
    w_query,
    w_key,
    w_value,
    w_beta,
    beta_max,
    out_gain,
    clip_lengths,
    delay_offsets,
    block_order,
):
    Z, X, H = dims["Z"], dims["X"], dims["H"]
    F, W = dims["F"], dims["W"]
    G = X * CORES
    BR = F // (Z * G)
    N = 128
    count = 128
    vmem, smem, anyw = (
        pl.BlockSpec(memory_space=s) for s in (pltpu.VMEM, pltpu.SMEM, pl.ANY)
    )
    D = w_query.shape[0]
    scratch = [
        pltpu.VMEM((D, W), BF16),
        pltpu.VMEM((D, W), BF16),
        pltpu.VMEM((D, W), BF16),
        pltpu.VMEM((2, F, N), BF16),
        pltpu.VMEM((G, Z * BR, W), BF16),
        pltpu.VMEM((G, Z * BR, W), BF16),
        pltpu.VMEM((Z, G * BR, W), BF16),
        pltpu.VMEM((Z, G * BR, W), BF16),
        pltpu.VMEM((16, W), BF16),
        pltpu.VMEM((16, W), BF16),
        pltpu.VMEM((H, F, W), BF16),
        pltpu.VMEM((F, 3 * W + 128), F32),
        pltpu.VMEM((2, F, 4 * N), F32),
        pltpu.VMEM((2, F, 4 * N), F32),
        pltpu.VMEM((X, N, 2 * N), BF16),
        pltpu.VMEM((N, 2 * N), BF16),
        pltpu.VMEM((N, 2 * N), BF16),
        pltpu.VMEM((N, N), BF16),
        pltpu.VMEM((N, N), BF16),
        pltpu.VMEM((2, F, N), BF16),
        pltpu.VMEM((2, F, N), BF16),
        pltpu.VMEM((X, N, N), BF16),
        pltpu.VMEM((N, N), BF16),
        pltpu.VMEM((N, N), BF16),
        pltpu.VMEM((N, N), BF16),
        pltpu.VMEM((2, F, 4 * N), BF16),
        pltpu.VMEM((2, F, 4 * N), BF16),
        pltpu.VMEM((8, F, W), BF16),
        pltpu.VMEM((8, F, W), BF16),
        pltpu.VMEM((F, W), BF16),
        pltpu.VMEM((16, W), BF16),
        pltpu.SemaphoreType.DMA((4,)),
        pltpu.SemaphoreType.DMA((count,)),
        pltpu.SemaphoreType.DMA((count,)),
    ]
    result = pl.pallas_call(
        functools.partial(kernel, dims),
        out_shape=jax.ShapeDtypeStruct((2, F, W), BF16),
        in_specs=[vmem, anyw, anyw, anyw, anyw, vmem, smem, vmem, smem, smem, vmem],
        out_specs=vmem,
        scratch_shapes=scratch,
        compiler_params=pltpu.CompilerParams(
            collective_id=0, has_side_effects=True, vmem_limit_bytes=60 * 2**20
        ),
    )(
        loaded,
        out_grad,
        w_query,
        w_key,
        w_value,
        w_beta.T,
        beta_max,
        out_gain.reshape(1, -1),
        clip_lengths,
        delay_offsets,
        block_order,
    )
    return result[0], result[1]


def build(mesh, chips_x, frames):
    seq, head = mesh.shape["seq"], mesh.shape["head"]
    dims = dict(Z=seq // (chips_x * CORES), X=chips_x, H=head, F=frames, W=256)
    return jax.shard_map(
        functools.partial(on_device, dims),
        mesh=mesh,
        in_specs=(
            P("seq", "head"),
            P("seq", "head"),
            P(None, "head"),
            P(None, "head"),
            P(None, "head"),
            P(None, "head"),
            P("head"),
            P(),
            P(),
            P(),
            P("seq", None),
        ),
        out_specs=(P("seq", "head"), P("seq", "head")),
        check_vma=False,
    )


def solution(mesh):
    return build(mesh, CHIPS_X, 128)
```

```python
import functools

import jax
import jax.numpy as jnp
from jax import lax
from jax.experimental import pallas as pl
from jax.experimental.pallas import tpu as pltpu
from jax.sharding import PartitionSpec as P

EPSILON = 1e-06
F32, BF16 = jnp.float32, jnp.bfloat16
CORES = 2
CHIPS_X = 4

NN = (1, 0)
NT = (1, 1)
TN = (0, 0)


def dot(a, b, kind=NN):
    return lax.dot_general(
        a, b, (((kind[0],), (kind[1],)), ((), ())), preferred_element_type=F32
    )


def split(x):
    high = x.astype(BF16)
    return high, (x - high.astype(F32)).astype(BF16)


def mm3(a, b, kind=NN):
    ah, al = split(a)
    bh, bl = split(b)
    return dot(
        jnp.concatenate([ah, ah, al], axis=kind[0]),
        jnp.concatenate([bh, bl, bh], axis=kind[1]),
        kind,
    )


def mm2(a, b, kind=NN):
    bh, bl = split(b)
    return dot(
        jnp.concatenate([a, a], axis=kind[0]), jnp.concatenate([bh, bl], axis=kind[1]), kind
    )


def mm1(a, b, kind=NN):
    return dot(a.astype(BF16), b.astype(BF16), kind)


def one_hot(condition):
    return jnp.where(condition, 1.0, 0.0).astype(BF16)


def iota(shape, dim):
    return lax.broadcasted_iota(jnp.int32, shape, dim)


def clip_start(lengths, positions):
    begin = jnp.zeros_like(positions)
    end = jnp.int32(0)
    for c in range(lengths.shape[0]):
        size = lengths[c]
        end = end + size
        begin = begin + jnp.where(end <= positions, size, 0)
    return begin


def kernel(
    dims,
    loaded_hbm,
    out_grad,
    w_query,
    w_key,
    w_value,
    w_beta_hbm,
    beta_max_hbm,
    out_gain_hbm,
    clip_lengths_hbm,
    delay_offsets_hbm,
    block_order_hbm,
    both_out,
    loaded,
    w_beta,
    beta_max,
    out_gain,
    clip_lengths,
    delay_offsets,
    block_order,
    wq,
    wk,
    wv,
    cot,
    s1,
    r1,
    s2,
    r2,
    last,
    tail,
    feat,
    acc,
    raw,
    pair_raw,
    plane,
    group,
    from_z1,
    from_z2,
    a_next,
    out_pair,
    out_heads,
    gplane,
    ggroup,
    gz1,
    gz2,
    grad_pair,
    grad_heads,
    rs_send,
    rs_recv,
    summed,
    follow,
    summed_out,
    local_sem,
    send_sem,
    recv_sem,
):
    Z, X, H, F, W = dims["Z"], dims["X"], dims["H"], dims["F"], dims["W"]
    C = CORES
    G = X * C
    S = Z * G
    BR = F // S
    N = 128
    CB = delay_offsets.shape[0]
    seq, y = lax.axis_index("seq"), lax.axis_index("head")
    z = lax.div(seq, G)
    g = lax.rem(seq, G)
    x = lax.div(g, C)
    core = lax.rem(g, C)
    other = 1 - core

    def at(zz, gg):
        return (zz * G + gg, y)

    counter = [0]
    started = []

    def remote(src, dst, device, index=None):
        if index is None:
            index = counter[0]
            counter[0] += 1
        return pltpu.make_async_remote_copy(
            src_ref=src,
            dst_ref=dst,
            send_sem=send_sem.at[index],
            recv_sem=recv_sem.at[index],
            device_id=device,
            device_id_type=pl.DeviceIdType.MESH,
        )

    def go(copy):
        copy.start()
        started.append(copy)
        return copy

    fetches = [
        pltpu.make_async_copy(src, dst, local_sem.at[i])
        for i, (src, dst) in enumerate(
            ((w_query, wq), (w_key, wk), (w_value, wv))
        )
    ]
    partners = [at(lax.rem(z + k, Z), g) for k in range(1, Z)]
    partners += [at(z, lax.rem(g + k, G)) for k in range(1, G)]
    partners += [(lax.rem(seq + 1, S), y), (lax.rem(seq + S - 1, S), y)]
    partners += [(seq, lax.rem(y + k, H)) for k in range(1, H)]
    barrier = pltpu.get_barrier_semaphore()
    for partner in partners:
        pl.semaphore_signal(barrier, inc=1, device_id=partner, device_id_type=pl.DeviceIdType.MESH)
    small = [
        pltpu.make_async_copy(src, dst, local_sem.at[4 + i])
        for i, (src, dst) in enumerate(
            (
                (loaded_hbm, loaded),
                (clip_lengths_hbm, clip_lengths),
                (delay_offsets_hbm, delay_offsets),
                (block_order_hbm, block_order),
                (beta_max_hbm, beta_max),
                (out_gain_hbm, out_gain),
                (w_beta_hbm, w_beta),
            )
        )
    ]
    for copy in small:
        copy.start()

    rows1, zbr = G * BR, Z * BR
    row, col = iota((F, F), 0), iota((F, F), 1)
    to_g, to_z = row // zbr, (row % zbr) // BR
    regroup = one_hot(col == to_z * rows1 + to_g * BR + row % BR)
    small[0].wait()
    s1[...] = dot(regroup, loaded[...]).astype(BF16).reshape(G, zbr, W)
    pl.semaphore_wait(barrier, len(partners))
    copies = []
    for k in range(1, G):
        to = lax.rem(g + k, G)
        copies.append(go(remote(s1.at[to], r1.at[g], at(z, to))))
    r1[g] = s1[g]
    sibling = at(z, x * C + other)

    def head_columns(h):
        return out_grad.at[:, pl.ds(pl.multiple_of(h * N, N), N)]

    cot_copy = go(remote(head_columns(other), cot.at[core], sibling))
    cot_keep = pltpu.make_async_copy(head_columns(core), cot.at[core], local_sem.at[3])
    cot_keep.start()
    for copy in fetches:
        copy.start()

    for copy in small[1:]:
        copy.wait()
    first = seq * F
    pos_col = first + iota((F, 1), 0)
    begin_col = clip_start(clip_lengths, pos_col)
    delay = delay_offsets[lax.div(y * CB, H)]
    eye = jnp.where(row == col, 1.0, 0.0)
    low, low_eq, carried, final, carried_last = ([] for _ in range(5))
    for i in range(C):
        start = (seq - core + i) * F
        at_col = clip_start(clip_lengths, start + iota((F, 1), 0))
        at_row = clip_start(clip_lengths, start + iota((1, F), 1))
        same = jnp.where(at_col == at_row, 1.0, 0.0)
        low.append(jnp.where(row > col, same, 0.0))
        low_eq.append(jnp.where(row >= col, same, 0.0))
        carried.append(jnp.where(at_col < start, 1.0, 0.0))
        final.append(jnp.where(at_col == at_col[F - 1 : F, :], 1.0, 0.0))
        carried_last.append(carried[i][F - 1 : F, :])

    order = jnp.broadcast_to(block_order[...], (16, S)).astype(F32).astype(BF16)
    spread = one_hot(iota((S, F), 0) == iota((S, F), 1) // BR)
    target = dot(order, spread)[0:1, :].astype(jnp.int32) * BR + iota((1, F), 1) % BR
    place = one_hot(row == target)
    to_g, to_z = (row % rows1) // BR, row // rows1
    back_to_z = one_hot(col == to_g * zbr + to_z * BR + row % BR)

    for copy in copies:
        copy.wait_recv()
    s2[...] = dot(back_to_z, r1[...].reshape(F, W)).astype(BF16).reshape(Z, rows1, W)
    copies = []
    for k in range(1, Z):
        to = lax.rem(z + k, Z)
        copies.append(go(remote(s2.at[to], r2.at[z], at(to, g))))
    r2[z] = s2[z]
    for copy in copies:
        copy.wait_recv()
    arranged = dot(place, r2[...].reshape(F, W)).astype(BF16)
    last[...] = arranged[F - 16 :, :]

    half = F // 2
    chunks = ((half, F), (16, half), (0, 16))

    def ring(k):
        return lax.rem(y + k + H, H)

    def along(k):
        return (seq, ring(k))

    halo = go(remote(last, tail, (lax.rem(seq + 1, S), y)))
    source = jnp.where(pos_col - delay >= begin_col, iota((F, 1), 0) - delay, -100)
    direct = {}

    def send_own(b):
        own = feat.at[y, pl.ds(chunks[b][0], chunks[b][1] - chunks[b][0])]
        for k in (2, -2, 1, -1):
            direct[k, b] = go(remote(own, own, along(k)))

    shift = one_hot(source == iota((F, F), 1))
    feat[y, half:, :] = dot(shift[half:, :], arranged).astype(BF16)
    send_own(0)
    early = dot(shift[:half, :], arranged)
    feat[y, 16:half, :] = early[16:, :].astype(BF16)
    send_own(1)
    halo.wait_recv()
    shift = one_hot(source[:16, :] == iota((16, 16), 1) - 16)
    feat[y, 0:16, :] = (early[:16, :] + dot(shift, tail[...])).astype(BF16)
    send_own(2)

    def project(owner, begin):
        block = feat[owner]
        here = pl.ds(pl.multiple_of(owner * W, W), W)
        for i, weight in enumerate((wq, wk, wv)):
            value = dot(block, weight[here, :])
            at_cols = slice(i * W, (i + 1) * W)
            acc[:, at_cols] = value if begin else acc[:, at_cols] + value
        value = dot(block, w_beta[:, here], NT)
        acc[:, 3 * W : 3 * W + 2] = value if begin else acc[:, 3 * W : 3 * W + 2] + value

    for copy in fetches:
        copy.wait()
    project(y, True)
    relays = {}
    for b in range(3):
        for d in (1, -1):
            direct[2 * d, b].wait_recv()
            block = feat.at[ring(-2 * d), pl.ds(chunks[b][0], chunks[b][1] - chunks[b][0])]
            relays[3 * d, b] = go(remote(block, block, along(d)))
            if (b == 0) == (d == 1):
                relays[4 * d, b] = go(remote(block, block, along(2 * d)))
    for k in (2, -2, 1, -1):
        if k in (1, -1):
            for b in range(3):
                direct[k, b].wait_recv()
        project(ring(-k), False)
    for k in (3, -3):
        for b in range(3):
            relays[k, b].wait_recv()
        project(ring(-k), False)
    for k, b in ((4, 0), (-4, 1), (-4, 2)):
        relays[k, b].wait_recv()
    project(ring(4), False)

    for h in range(C):
        for i in range(3):
            raw[h, :, i * N : (i + 1) * N] = acc[:, i * W + h * N : i * W + (h + 1) * N]
        raw[h, :, 3 * N :] = jnp.broadcast_to(acc[:, 3 * W + h : 3 * W + h + 1], (F, N))
    copy = go(remote(raw.at[other], pair_raw.at[core], sibling))
    pair_raw[core] = raw[core]
    copy.wait_recv()

    both_cores = range(C)
    Q, K, V, beta, nq, nk, sig, Gm, T = ({} for _ in range(9))
    for h in both_cores:
        q_raw, k_raw = pair_raw[h, :, :N], pair_raw[h, :, N : 2 * N]
        V[h] = pair_raw[h, :, 2 * N : 3 * N]
        nq[h] = lax.rsqrt(jnp.sum(q_raw * q_raw, axis=1, keepdims=True) + EPSILON)
        nk[h] = lax.rsqrt(jnp.sum(k_raw * k_raw, axis=1, keepdims=True) + EPSILON)
        Q[h], K[h] = q_raw * nq[h], k_raw * nk[h]
        sig[h] = 1.0 / (1.0 + jnp.exp(-pair_raw[h, :, 3 * N : 3 * N + 1]))
        beta[h] = beta_max[core] * sig[h]
    L = {}
    for h in both_cores:
        Gm[h] = mm3(K[h], K[h], NT) * low[h]
        L[h] = beta[h] * Gm[h]
    size = 1
    while size < F:
        pair = (
            ((row // (2 * size)) == (col // (2 * size)))
            & ((row // size) % 2 == 1)
            & ((col // size) % 2 == 0)
        )
        inner = {h: jnp.where(pair, L[h], 0.0) for h in both_cores}
        if size == 1:
            T = {h: eye - inner[h] for h in both_cores}
        else:
            half_way = {h: mm3(T[h], inner[h]) for h in both_cores}
            T = {h: T[h] - mm3(half_way[h], T[h]) for h in both_cores}
        size *= 2
    Wk, Wv, A, B = {}, {}, {}, {}
    for h in both_cores:
        both = mm3(T[h], beta[h] * jnp.concatenate([K[h], V[h]], axis=1))
        Wk[h], Wv[h] = both[:, :N], both[:, N:]
    for h in both_cores:
        both = mm3(K[h], jnp.concatenate([Wk[h], final[h] * Wv[h]], axis=1), TN)
        A[h] = carried_last[h] * (eye - both[:, :N])
        B[h] = both[:, N:]

    zero = jnp.zeros((N, N), F32)
    pad_b = jnp.concatenate([zero, B[1]], axis=1)
    plane[x] = (mm3(A[1], jnp.concatenate([A[0], B[0]], axis=1)) + pad_b).astype(BF16)
    copies = []
    for k in range(1, X):
        to = lax.rem(x + k, X)
        copies.append(go(remote(plane.at[x], plane.at[x], at(z, to * C + core))))
    P_, Oloc, R = {}, {}, {}
    for h in both_cores:
        P_[h] = mm3(Q[h], K[h], NT) * low_eq[h]
        both = mm3(P_[h], jnp.concatenate([carried[h] * Wk[h], Wv[h]], axis=1))
        R[h] = carried[h] * Q[h] - both[:, :N]
        Oloc[h] = both[:, N:]
    for copy in copies:
        copy.wait_recv()

    def then(before, after):
        shift = jnp.concatenate([zero, after[:, N:].astype(F32)], axis=1)
        return mm2(after[:, :N], before) + shift

    def then32(before, after):
        shift = jnp.concatenate([zero, after[:, N:]], axis=1)
        return mm3(after[:, :N], before) + shift

    maps = [plane[i] for i in range(X)]
    identity = jnp.concatenate([eye, zero], axis=1)
    prefix = [identity, maps[0].astype(F32)]
    if X == 4:
        front = then(prefix[1], maps[1])
        back = then(maps[2].astype(F32), maps[3])
        total = then32(front, back)
        prefix += [front]
    else:
        for i in range(1, X):
            total = then(prefix[-1], maps[i])
            prefix.append(total)
    group[...] = total.astype(BF16)
    z1, z2 = lax.rem(z + 1, Z), lax.rem(z + 2, Z)
    y1, y2 = lax.rem(z + Z - 1, Z), lax.rem(z + Z - 2, Z)
    copies = [
        go(remote(group, from_z1, at(z1, g))),
        go(remote(group.at[:, pl.ds(N, N)], from_z2, at(z2, g))),
    ]
    next_copy = go(remote(group.at[:, pl.ds(0, N)], a_next, at(y1, g)))
    if X == 4:
        prefix.append(then(front, maps[2]))
        a1, a2, a3 = (maps[i][:, :N] for i in (1, 2, 3))
        suffix = [mm2(a3, mm2(a2, a1.astype(F32))), back[:, :N], a3.astype(F32), eye]
    else:
        suffix = [eye]
        for i in range(X - 1, 0, -1):
            suffix.insert(0, mm3(suffix[0], maps[i][:, :N].astype(F32)))

    def pick(options, index):
        value = options[0]
        for i in range(1, len(options)):
            value = jnp.where(index == i, options[i], value)
        return value

    before_me = pick(prefix[:X], x)
    after_me = pick(suffix, x)
    for copy in copies:
        copy.wait_recv()
    s_group = from_z1[:, N:].astype(F32) + dot(from_z1[:, :N], from_z2[...])
    s_chip = before_me[:, N:] + mm3(before_me[:, :N], s_group)
    state = (s_chip, B[0] + mm3(A[0], s_chip))

    gain = out_gain[...]
    O, dO, ask = {}, {}, {}
    cot_copy.wait_recv()
    cot_keep.wait()
    for h in both_cores:
        O[h] = Oloc[h] + mm3(R[h], state[h])
        inv = lax.rsqrt(jnp.mean(O[h] * O[h], axis=1, keepdims=True) + EPSILON)
        out_pair[h] = (O[h] * inv * gain).astype(BF16)
        scaled = cot[h].astype(F32) * gain
        unit = O[h] * inv
        dO[h] = inv * (scaled - unit * jnp.mean(scaled * unit, axis=1, keepdims=True))
        ask[h] = mm3(R[h], dO[h], TN)
    gplane[x] = (ask[0] + mm3(A[0], ask[1], TN)).astype(BF16)
    copies = []
    for k in range(1, X):
        to = lax.rem(x + k, X)
        copies.append(go(remote(gplane.at[x], gplane.at[x], at(z, to * C + core))))
    out_copy = go(remote(out_pair.at[other], out_heads.at[core], sibling))
    out_heads[core] = out_pair[core]
    U, dU0, Y, dX0, dP, dQ, dK0, Zv = ({} for _ in range(8))
    for h in both_cores:
        Zv[h] = V[h] - carried[h] * mm3(K[h], state[h])
        U[h] = Wv[h] - carried[h] * mm3(Wk[h], state[h])
        dU0[h] = mm3(P_[h], dO[h], TN)
        both = mm3(T[h], jnp.concatenate([dU0[h], final[h] * K[h]], axis=1), TN)
        dX0[h], Y[h] = both[:, :N], both[:, N:]
    for copy in copies:
        copy.wait_recv()
    gs = [gplane[i].astype(F32) for i in range(X)]

    def back_through(i, later):
        return gs[i] + mm2(maps[i][:, :N], later, TN)

    if X == 4:
        pair_late = back_through(2, gs[3])
        pair_early = back_through(0, gs[1])
        g_total = pair_early + mm3(front[:, :N], pair_late, TN)
        behind = [back_through(1, pair_late), pair_late, gs[3], zero]
    else:
        behind = [zero]
        for i in range(X - 1, -1, -1):
            behind.insert(0, back_through(i, behind[0]))
        g_total = behind[0]
        behind = behind[1:]
    ggroup[...] = g_total.astype(BF16)
    copies = [
        go(remote(ggroup, gz1, at(y1, g))),
        go(remote(ggroup, gz2, at(y2, g))),
    ]
    behind_me = pick(behind, x)
    for h in both_cores:
        dP[h] = mm3(dO[h], U[h], NT) * low_eq[h]
        dQ[h] = carried[h] * mm3(dO[h], state[h], NT) + mm3(dP[h], K[h])
        dK0[h] = mm3(dP[h], Q[h], TN)
        grad = nq[h] * (dQ[h] - Q[h] * jnp.sum(Q[h] * dQ[h], axis=1, keepdims=True))
        grad_pair[h, :, :N] = grad.astype(BF16)
    out_copy.wait_recv()
    head_outs = [
        pltpu.make_async_copy(
            out_heads.at[h], both_out.at[0, :, pl.ds(h * N, N)], local_sem.at[12 + h]
        )
        for h in range(C)
    ]
    for copy in head_outs:
        copy.start()
    next_copy.wait_recv()
    for copy in copies:
        copy.wait_recv()
    d_group = gz1[...].astype(F32) + dot(a_next[...], gz2[...], TN)
    d_chip = behind_me + mm3(after_me, d_group, TN)
    d_state = (ask[1] + mm3(A[1], d_chip, TN), d_chip)

    for h in both_cores:
        dX = dX0[h] + mm3(Y[h], d_state[h])
        both = mm3(dX, jnp.concatenate([U[h], state[h]], axis=0), NT)
        dL = -both[:, :F] * low[h]
        dG = beta[h] * dL
        dK = dK0[h] + mm3(final[h] * U[h], d_state[h], NT)
        dK = dK - carried[h] * beta[h] * both[:, F:]
        dK = dK + mm3(dG, K[h]) + mm3(dG, K[h], TN)
        d_beta = jnp.sum(dX * Zv[h], axis=1, keepdims=True)
        d_beta = d_beta + jnp.sum(dL * Gm[h], axis=1, keepdims=True)
        grad = nk[h] * (dK - K[h] * jnp.sum(K[h] * dK, axis=1, keepdims=True))
        d_logit = d_beta * beta[h] * (1.0 - sig[h])
        grad_pair[h, :, N : 2 * N] = grad.astype(BF16)
        grad_pair[h, :, 2 * N : 3 * N] = (beta[h] * dX).astype(BF16)
        grad_pair[h, :, 3 * N :] = jnp.broadcast_to(d_logit, (F, N)).astype(BF16)
    copy = go(remote(grad_pair.at[other], grad_heads.at[core], sibling))
    grad_heads[core] = grad_pair[core]
    copy.wait_recv()
    wide = [
        jnp.concatenate([grad_heads[h, :, i * N : (i + 1) * N] for h in range(C)], axis=1)
        for i in range(3)
    ]
    dlog = [grad_heads[h, :, 3 * N : 3 * N + 1].astype(F32) for h in range(C)]

    def partial(owner):
        here = pl.ds(pl.multiple_of(owner * W, W), W)
        rows = w_beta[:, here].astype(F32)
        value = dlog[0] * rows[0:1, :] + dlog[1] * rows[1:2, :]
        for i, weight in enumerate((wq, wk, wv)):
            value = value + dot(wide[i], weight[here, :], NT)
        return value

    hop = (-1, 1, -2, 2, -1, 1, -2, 2)
    parts = {}

    chunks = ((0, 16), (16, half), (half, F))

    def send_rows(kind, b, value):
        rows = pl.ds(chunks[b][0], chunks[b][1] - chunks[b][0])
        src, dst = rs_send.at[kind, rows], rs_recv.at[kind, rows]
        if kind in (2, 3):
            src, dst = src.at[:, pl.ds(0, N)], dst.at[:, pl.ds(0, N)]
            rs_send[kind, rows, :N] = value.astype(BF16)
        else:
            rs_send[kind, rows] = value.astype(BF16)
        reduces[kind, b] = go(remote(src, dst, along(hop[kind])))

    def rows_of(k, b):
        return parts[k][chunks[b][0] : chunks[b][1], :]

    def received(kind, b):
        reduces[kind, b].wait_recv()
        return rs_recv[kind, chunks[b][0] : chunks[b][1], :]

    reduces = {}
    for k in (-3, 3, 4):
        parts[k] = partial(ring(k))
    for b in range(3):
        send_rows(0, b, rows_of(-3, b))
        send_rows(1, b, rows_of(3, b))
        send_rows(2, b, rows_of(4, b)[:, :N])
        send_rows(3, b, rows_of(4, b)[:, N:])
    for k in (-1, 1):
        parts[k] = partial(ring(k))
    for b in range(3):
        send_rows(4, b, rows_of(-1, b))
        send_rows(5, b, rows_of(1, b))
    for k in (-2, 2, 0):
        parts[k] = partial(ring(k))

    def hand_on(b):
        for kind, k in ((6, -2), (7, 2)):
            value = rows_of(k, b) + received(kind - 6, b).astype(F32)
            extra = received(kind - 4, b)[:, :N].astype(F32)
            blank = jnp.zeros_like(extra)
            extra = jnp.concatenate([extra, blank] if kind == 6 else [blank, extra], axis=1)
            send_rows(kind, b, value + extra)

    def finish_rows(b):
        value = rows_of(0, b)
        for kind in (4, 5, 6, 7):
            value = value + received(kind, b).astype(F32)
        summed[chunks[b][0] : chunks[b][1], :] = value.astype(BF16)

    for b in range(3):
        hand_on(b)
    for b in range(3):
        finish_rows(b)
        if b == 0:
            halo = go(remote(summed.at[pl.ds(0, 16)], follow, (lax.rem(seq + S - 1, S), y)))
    ahead = pos_col + delay
    reaches = (ahead < S * F) & (clip_start(clip_lengths, ahead) <= pos_col)
    wanted = jnp.where(reaches, ahead - first, -1)
    pull = one_hot(wanted == iota((F, F + 16), 1))
    halo.wait_recv()
    both = jnp.concatenate([summed[...], follow[...]], axis=0)
    summed_out[...] = dot(pull, both).astype(BF16)
    last_out = pltpu.make_async_copy(summed_out, both_out.at[1], local_sem.at[11])
    last_out.start()
    for copy in started:
        copy.wait_send()
    for copy in head_outs:
        copy.wait()
    last_out.wait()


def on_device(
    dims,
    loaded,
    out_grad,
    w_query,
    w_key,
    w_value,
    w_beta,
    beta_max,
    out_gain,
    clip_lengths,
    delay_offsets,
    block_order,
):
    Z, X, H = dims["Z"], dims["X"], dims["H"]
    F, W = dims["F"], dims["W"]
    G = X * CORES
    BR = F // (Z * G)
    N = 128
    count = 128
    anyw = pl.BlockSpec(memory_space=pl.ANY)
    D = w_query.shape[0]
    scratch = [
        pltpu.VMEM((F, W), BF16),
        pltpu.VMEM((2, D), BF16),
        pltpu.SMEM(beta_max.shape, F32),
        pltpu.VMEM((1, N), F32),
        pltpu.SMEM(clip_lengths.shape, jnp.int32),
        pltpu.SMEM(delay_offsets.shape, jnp.int32),
        pltpu.VMEM(block_order.shape, jnp.int32),
        pltpu.VMEM((D, W), BF16),
        pltpu.VMEM((D, W), BF16),
        pltpu.VMEM((D, W), BF16),
        pltpu.VMEM((2, F, N), BF16),
        pltpu.VMEM((G, Z * BR, W), BF16),
        pltpu.VMEM((G, Z * BR, W), BF16),
        pltpu.VMEM((Z, G * BR, W), BF16),
        pltpu.VMEM((Z, G * BR, W), BF16),
        pltpu.VMEM((16, W), BF16),
        pltpu.VMEM((16, W), BF16),
        pltpu.VMEM((H, F, W), BF16),
        pltpu.VMEM((F, 3 * W + 128), F32),
        pltpu.VMEM((2, F, 4 * N), F32),
        pltpu.VMEM((2, F, 4 * N), F32),
        pltpu.VMEM((X, N, 2 * N), BF16),
        pltpu.VMEM((N, 2 * N), BF16),
        pltpu.VMEM((N, 2 * N), BF16),
        pltpu.VMEM((N, N), BF16),
        pltpu.VMEM((N, N), BF16),
        pltpu.VMEM((2, F, N), BF16),
        pltpu.VMEM((2, F, N), BF16),
        pltpu.VMEM((X, N, N), BF16),
        pltpu.VMEM((N, N), BF16),
        pltpu.VMEM((N, N), BF16),
        pltpu.VMEM((N, N), BF16),
        pltpu.VMEM((2, F, 4 * N), BF16),
        pltpu.VMEM((2, F, 4 * N), BF16),
        pltpu.VMEM((8, F, W), BF16),
        pltpu.VMEM((8, F, W), BF16),
        pltpu.VMEM((F, W), BF16),
        pltpu.VMEM((16, W), BF16),
        pltpu.VMEM((F, W), BF16),
        pltpu.SemaphoreType.DMA((16,)),
        pltpu.SemaphoreType.DMA((count,)),
        pltpu.SemaphoreType.DMA((count,)),
    ]
    result = pl.pallas_call(
        functools.partial(kernel, dims),
        out_shape=jax.ShapeDtypeStruct((2, F, W), BF16),
        in_specs=[anyw] * 11,
        out_specs=anyw,
        scratch_shapes=scratch,
        compiler_params=pltpu.CompilerParams(
            collective_id=0, has_side_effects=True, vmem_limit_bytes=60 * 2**20
        ),
    )(
        loaded,
        out_grad,
        w_query,
        w_key,
        w_value,
        w_beta.T,
        beta_max,
        out_gain.reshape(1, -1),
        clip_lengths,
        delay_offsets,
        block_order,
    )
    return result[0], result[1]


def build(mesh, chips_x, frames):
    seq, head = mesh.shape["seq"], mesh.shape["head"]
    dims = dict(Z=seq // (chips_x * CORES), X=chips_x, H=head, F=frames, W=256)
    return jax.shard_map(
        functools.partial(on_device, dims),
        mesh=mesh,
        in_specs=(
            P("seq", "head"),
            P("seq", "head"),
            P(None, "head"),
            P(None, "head"),
            P(None, "head"),
            P(None, "head"),
            P("head"),
            P(),
            P(),
            P(),
            P("seq", None),
        ),
        out_specs=(P("seq", "head"), P("seq", "head")),
        check_vma=False,
    )


def solution(mesh):
    return build(mesh, CHIPS_X, 128)
```

```python
import functools

import jax
import jax.numpy as jnp
from jax import lax
from jax.experimental import pallas as pl
from jax.experimental.pallas import tpu as pltpu
from jax.sharding import PartitionSpec as P

EPSILON = 1e-06
F32, BF16 = jnp.float32, jnp.bfloat16
CORES = 2
CHIPS_X = 4

NN = (1, 0)
NT = (1, 1)
TN = (0, 0)


def dot(a, b, kind=NN):
    return lax.dot_general(
        a, b, (((kind[0],), (kind[1],)), ((), ())), preferred_element_type=F32
    )


def split(x):
    high = x.astype(BF16)
    return high, (x - high.astype(F32)).astype(BF16)


def mm3(a, b, kind=NN):
    ah, al = split(a)
    bh, bl = split(b)
    return dot(
        jnp.concatenate([ah, ah, al], axis=kind[0]),
        jnp.concatenate([bh, bl, bh], axis=kind[1]),
        kind,
    )


def mm2(a, b, kind=NN):
    bh, bl = split(b)
    return dot(
        jnp.concatenate([a, a], axis=kind[0]), jnp.concatenate([bh, bl], axis=kind[1]), kind
    )


def mm1(a, b, kind=NN):
    return dot(a.astype(BF16), b.astype(BF16), kind)


def one_hot(condition):
    return jnp.where(condition, 1.0, 0.0).astype(BF16)


def iota(shape, dim):
    return lax.broadcasted_iota(jnp.int32, shape, dim)


def clip_start(lengths, positions):
    begin = jnp.zeros_like(positions)
    end = jnp.int32(0)
    for c in range(lengths.shape[0]):
        size = lengths[c]
        end = end + size
        begin = begin + jnp.where(end <= positions, size, 0)
    return begin


def kernel(
    dims,
    loaded_hbm,
    out_grad,
    w_query,
    w_key,
    w_value,
    w_beta_hbm,
    beta_max_hbm,
    out_gain_hbm,
    clip_lengths_hbm,
    delay_offsets_hbm,
    block_order_hbm,
    both_out,
    loaded,
    w_beta,
    beta_max,
    out_gain,
    clip_lengths,
    delay_offsets,
    block_order,
    wq,
    wk,
    wv,
    cot,
    s1,
    r1,
    s2,
    r2,
    last,
    tail,
    feat,
    acc,
    raw,
    pair_raw,
    plane,
    group,
    from_z1,
    from_z2,
    a_next,
    out_pair,
    out_heads,
    gplane,
    ggroup,
    gz1,
    gz2,
    grad_pair,
    grad_heads,
    rs_send,
    rs_recv,
    summed,
    follow,
    summed_out,
    local_sem,
    send_sem,
    recv_sem,
):
    Z, X, H, F, W = dims["Z"], dims["X"], dims["H"], dims["F"], dims["W"]
    C = CORES
    G = X * C
    S = Z * G
    BR = F // S
    N = 128
    CB = delay_offsets.shape[0]
    seq, y = lax.axis_index("seq"), lax.axis_index("head")
    z = lax.div(seq, G)
    g = lax.rem(seq, G)
    x = lax.div(g, C)
    core = lax.rem(g, C)
    other = 1 - core

    def at(zz, gg):
        return (zz * G + gg, y)

    counter = [0]
    started = []

    def remote(src, dst, device, index=None):
        if index is None:
            index = counter[0]
            counter[0] += 1
        return pltpu.make_async_remote_copy(
            src_ref=src,
            dst_ref=dst,
            send_sem=send_sem.at[index],
            recv_sem=recv_sem.at[index],
            device_id=device,
            device_id_type=pl.DeviceIdType.MESH,
        )

    def go(copy):
        copy.start()
        started.append(copy)
        return copy

    fetches = [
        pltpu.make_async_copy(src, dst, local_sem.at[i])
        for i, (src, dst) in enumerate(
            ((w_query, wq), (w_key, wk), (w_value, wv))
        )
    ]
    partners = [at(lax.rem(z + k, Z), g) for k in range(1, Z)]
    partners += [at(z, lax.rem(g + k, G)) for k in range(1, G)]
    partners += [(lax.rem(seq + 1, S), y), (lax.rem(seq + S - 1, S), y)]
    partners += [(seq, lax.rem(y + k, H)) for k in range(1, H)]
    barrier = pltpu.get_barrier_semaphore()
    for partner in partners:
        pl.semaphore_signal(barrier, inc=1, device_id=partner, device_id_type=pl.DeviceIdType.MESH)
    small = [
        pltpu.make_async_copy(src, dst, local_sem.at[4 + i])
        for i, (src, dst) in enumerate(
            (
                (loaded_hbm, loaded),
                (clip_lengths_hbm, clip_lengths),
                (delay_offsets_hbm, delay_offsets),
                (block_order_hbm, block_order),
                (beta_max_hbm, beta_max),
                (out_gain_hbm, out_gain),
                (w_beta_hbm, w_beta),
            )
        )
    ]
    for copy in small:
        copy.start()

    rows1, zbr = G * BR, Z * BR
    row, col = iota((F, F), 0), iota((F, F), 1)
    to_g, to_z = row // zbr, (row % zbr) // BR
    regroup = one_hot(col == to_z * rows1 + to_g * BR + row % BR)
    small[0].wait()
    s1[...] = dot(regroup, loaded[...]).astype(BF16).reshape(G, zbr, W)
    pl.semaphore_wait(barrier, len(partners))
    copies = []
    for k in range(1, G):
        to = lax.rem(g + k, G)
        copies.append(go(remote(s1.at[to], r1.at[g], at(z, to))))
    r1[g] = s1[g]
    sibling = at(z, x * C + other)

    def head_columns(h):
        return out_grad.at[:, pl.ds(pl.multiple_of(h * N, N), N)]

    cot_copy = go(remote(head_columns(other), cot.at[core], sibling))
    cot_keep = pltpu.make_async_copy(head_columns(core), cot.at[core], local_sem.at[3])
    cot_keep.start()
    for copy in fetches:
        copy.start()

    for copy in small[1:]:
        copy.wait()
    first = seq * F
    pos_col = first + iota((F, 1), 0)
    begin_col = clip_start(clip_lengths, pos_col)
    delay = delay_offsets[lax.div(y * CB, H)]
    eye = jnp.where(row == col, 1.0, 0.0)
    low, low_eq, carried, final, carried_last = ([] for _ in range(5))
    for i in range(C):
        start = (seq - core + i) * F
        at_col = clip_start(clip_lengths, start + iota((F, 1), 0))
        at_row = clip_start(clip_lengths, start + iota((1, F), 1))
        same = jnp.where(at_col == at_row, 1.0, 0.0)
        low.append(jnp.where(row > col, same, 0.0))
        low_eq.append(jnp.where(row >= col, same, 0.0))
        carried.append(jnp.where(at_col < start, 1.0, 0.0))
        final.append(jnp.where(at_col == at_col[F - 1 : F, :], 1.0, 0.0))
        carried_last.append(carried[i][F - 1 : F, :])

    order = jnp.broadcast_to(block_order[...], (16, S)).astype(F32).astype(BF16)
    spread = one_hot(iota((S, F), 0) == iota((S, F), 1) // BR)
    target = dot(order, spread)[0:1, :].astype(jnp.int32) * BR + iota((1, F), 1) % BR
    place = one_hot(row == target)
    to_g, to_z = (row % rows1) // BR, row // rows1
    back_to_z = one_hot(col == to_g * zbr + to_z * BR + row % BR)

    for copy in copies:
        copy.wait_recv()
    s2[...] = dot(back_to_z, r1[...].reshape(F, W)).astype(BF16).reshape(Z, rows1, W)
    copies = []
    for k in range(1, Z):
        to = lax.rem(z + k, Z)
        copies.append(go(remote(s2.at[to], r2.at[z], at(to, g))))
    r2[z] = s2[z]
    for copy in copies:
        copy.wait_recv()
    arranged = dot(place, r2[...].reshape(F, W)).astype(BF16)
    last[...] = arranged[F - 16 :, :]

    half = F // 2
    chunks = ((half, F), (16, half), (0, 16))

    def ring(k):
        return lax.rem(y + k + H, H)

    def along(k):
        return (seq, ring(k))

    halo = go(remote(last, tail, (lax.rem(seq + 1, S), y)))
    source = jnp.where(pos_col - delay >= begin_col, iota((F, 1), 0) - delay, -100)
    direct = {}

    def send_own(b):
        own = feat.at[y, pl.ds(chunks[b][0], chunks[b][1] - chunks[b][0])]
        for k in (2, -2, 1, -1):
            direct[k, b] = go(remote(own, own, along(k)))

    shift = one_hot(source == iota((F, F), 1))
    feat[y, half:, :] = dot(shift[half:, :], arranged).astype(BF16)
    send_own(0)
    early = dot(shift[:half, :], arranged)
    feat[y, 16:half, :] = early[16:, :].astype(BF16)
    send_own(1)
    halo.wait_recv()
    shift = one_hot(source[:16, :] == iota((16, 16), 1) - 16)
    feat[y, 0:16, :] = (early[:16, :] + dot(shift, tail[...])).astype(BF16)
    send_own(2)

    def project(owner, begin):
        block = feat[owner]
        here = pl.ds(pl.multiple_of(owner * W, W), W)
        for i, weight in enumerate((wq, wk, wv)):
            value = dot(block, weight[here, :])
            at_cols = slice(i * W, (i + 1) * W)
            acc[:, at_cols] = value if begin else acc[:, at_cols] + value
        value = dot(block, w_beta[:, here], NT)
        acc[:, 3 * W : 3 * W + 2] = value if begin else acc[:, 3 * W : 3 * W + 2] + value

    for copy in fetches:
        copy.wait()
    project(y, True)
    relays = {}
    for b in range(3):
        for d in (1, -1):
            direct[2 * d, b].wait_recv()
            block = feat.at[ring(-2 * d), pl.ds(chunks[b][0], chunks[b][1] - chunks[b][0])]
            relays[3 * d, b] = go(remote(block, block, along(d)))
            if (b == 0) == (d == 1):
                relays[4 * d, b] = go(remote(block, block, along(2 * d)))
    for k in (2, -2, 1, -1):
        if k in (1, -1):
            for b in range(3):
                direct[k, b].wait_recv()
        project(ring(-k), False)
    for k in (3, -3):
        for b in range(3):
            relays[k, b].wait_recv()
        project(ring(-k), False)
    for k, b in ((4, 0), (-4, 1), (-4, 2)):
        relays[k, b].wait_recv()
    project(ring(4), False)

    for h in range(C):
        for i in range(3):
            raw[h, :, i * N : (i + 1) * N] = acc[:, i * W + h * N : i * W + (h + 1) * N]
        raw[h, :, 3 * N :] = jnp.broadcast_to(acc[:, 3 * W + h : 3 * W + h + 1], (F, N))
    copy = go(remote(raw.at[other], pair_raw.at[core], sibling))
    pair_raw[core] = raw[core]
    copy.wait_recv()

    both_cores = range(C)
    Q, K, V, beta, nq, nk, sig, Gm, T = ({} for _ in range(9))
    for h in both_cores:
        q_raw, k_raw = pair_raw[h, :, :N], pair_raw[h, :, N : 2 * N]
        V[h] = pair_raw[h, :, 2 * N : 3 * N]
        nq[h] = lax.rsqrt(jnp.sum(q_raw * q_raw, axis=1, keepdims=True) + EPSILON)
        nk[h] = lax.rsqrt(jnp.sum(k_raw * k_raw, axis=1, keepdims=True) + EPSILON)
        Q[h], K[h] = q_raw * nq[h], k_raw * nk[h]
        sig[h] = 1.0 / (1.0 + jnp.exp(-pair_raw[h, :, 3 * N : 3 * N + 1]))
        beta[h] = beta_max[core] * sig[h]
    L = {}
    for h in both_cores:
        Gm[h] = mm3(K[h], K[h], NT) * low[h]
        L[h] = beta[h] * Gm[h]
    size = 1
    while size < F:
        pair = (
            ((row // (2 * size)) == (col // (2 * size)))
            & ((row // size) % 2 == 1)
            & ((col // size) % 2 == 0)
        )
        inner = {h: jnp.where(pair, L[h], 0.0) for h in both_cores}
        if size == 1:
            T = {h: eye - inner[h] for h in both_cores}
        else:
            half_way = {h: mm3(T[h], inner[h]) for h in both_cores}
            T = {h: T[h] - mm3(half_way[h], T[h]) for h in both_cores}
        size *= 2
    Wk, Wv, A, B = {}, {}, {}, {}
    for h in both_cores:
        both = mm3(T[h], beta[h] * jnp.concatenate([K[h], V[h]], axis=1))
        Wk[h], Wv[h] = both[:, :N], both[:, N:]
    for h in both_cores:
        both = mm3(K[h], jnp.concatenate([Wk[h], final[h] * Wv[h]], axis=1), TN)
        A[h] = carried_last[h] * (eye - both[:, :N])
        B[h] = both[:, N:]

    zero = jnp.zeros((N, N), F32)
    pad_b = jnp.concatenate([zero, B[1]], axis=1)
    plane[x] = (mm3(A[1], jnp.concatenate([A[0], B[0]], axis=1)) + pad_b).astype(BF16)
    copies = []
    for k in range(1, X):
        to = lax.rem(x + k, X)
        copies.append(go(remote(plane.at[x], plane.at[x], at(z, to * C + core))))
    P_, Oloc, R = {}, {}, {}
    for h in both_cores:
        P_[h] = mm3(Q[h], K[h], NT) * low_eq[h]
        both = mm3(P_[h], jnp.concatenate([carried[h] * Wk[h], Wv[h]], axis=1))
        R[h] = carried[h] * Q[h] - both[:, :N]
        Oloc[h] = both[:, N:]
    for copy in copies:
        copy.wait_recv()

    def then(before, after):
        shift = jnp.concatenate([zero, after[:, N:].astype(F32)], axis=1)
        return mm2(after[:, :N], before) + shift

    def then32(before, after):
        shift = jnp.concatenate([zero, after[:, N:]], axis=1)
        return mm3(after[:, :N], before) + shift

    maps = [plane[i] for i in range(X)]
    identity = jnp.concatenate([eye, zero], axis=1)
    prefix = [identity, maps[0].astype(F32)]
    if X == 4:
        front = then(prefix[1], maps[1])
        back = then(maps[2].astype(F32), maps[3])
        total = then32(front, back)
        prefix += [front]
    else:
        for i in range(1, X):
            total = then(prefix[-1], maps[i])
            prefix.append(total)
    group[...] = total.astype(BF16)
    z1, z2 = lax.rem(z + 1, Z), lax.rem(z + 2, Z)
    y1, y2 = lax.rem(z + Z - 1, Z), lax.rem(z + Z - 2, Z)
    copies = [
        go(remote(group, from_z1, at(z1, g))),
        go(remote(group.at[:, pl.ds(N, N)], from_z2, at(z2, g))),
    ]
    next_copy = go(remote(group.at[:, pl.ds(0, N)], a_next, at(y1, g)))
    if X == 4:
        prefix.append(then(front, maps[2]))
        a1, a2, a3 = (maps[i][:, :N] for i in (1, 2, 3))
        suffix = [mm2(a3, mm2(a2, a1.astype(F32))), back[:, :N], a3.astype(F32), eye]
    else:
        suffix = [eye]
        for i in range(X - 1, 0, -1):
            suffix.insert(0, mm3(suffix[0], maps[i][:, :N].astype(F32)))

    def pick(options, index):
        value = options[0]
        for i in range(1, len(options)):
            value = jnp.where(index == i, options[i], value)
        return value

    before_me = pick(prefix[:X], x)
    after_me = pick(suffix, x)
    for copy in copies:
        copy.wait_recv()
    s_group = from_z1[:, N:].astype(F32) + dot(from_z1[:, :N], from_z2[...])
    s_chip = before_me[:, N:] + mm3(before_me[:, :N], s_group)
    state = (s_chip, B[0] + mm3(A[0], s_chip))

    gain = out_gain[...]
    O, dO, ask = {}, {}, {}
    cot_copy.wait_recv()
    cot_keep.wait()
    for h in both_cores:
        O[h] = Oloc[h] + mm3(R[h], state[h])
        inv = lax.rsqrt(jnp.mean(O[h] * O[h], axis=1, keepdims=True) + EPSILON)
        out_pair[h] = (O[h] * inv * gain).astype(BF16)
        scaled = cot[h].astype(F32) * gain
        unit = O[h] * inv
        dO[h] = inv * (scaled - unit * jnp.mean(scaled * unit, axis=1, keepdims=True))
        ask[h] = mm3(R[h], dO[h], TN)
    gplane[x] = (ask[0] + mm3(A[0], ask[1], TN)).astype(BF16)
    copies = []
    for k in range(1, X):
        to = lax.rem(x + k, X)
        copies.append(go(remote(gplane.at[x], gplane.at[x], at(z, to * C + core))))
    out_copy = go(remote(out_pair.at[other], out_heads.at[core], sibling))
    out_heads[core] = out_pair[core]
    U, dU0, Y, dX0, dP, dQ, dK0, Zv = ({} for _ in range(8))
    for h in both_cores:
        Zv[h] = V[h] - carried[h] * mm3(K[h], state[h])
        U[h] = Wv[h] - carried[h] * mm3(Wk[h], state[h])
        dU0[h] = mm3(P_[h], dO[h], TN)
        both = mm3(T[h], jnp.concatenate([dU0[h], final[h] * K[h]], axis=1), TN)
        dX0[h], Y[h] = both[:, :N], both[:, N:]
    for copy in copies:
        copy.wait_recv()
    gs = [gplane[i].astype(F32) for i in range(X)]

    def back_through(i, later):
        return gs[i] + mm2(maps[i][:, :N], later, TN)

    if X == 4:
        pair_late = back_through(2, gs[3])
        pair_early = back_through(0, gs[1])
        g_total = pair_early + mm3(front[:, :N], pair_late, TN)
        behind = [back_through(1, pair_late), pair_late, gs[3], zero]
    else:
        behind = [zero]
        for i in range(X - 1, -1, -1):
            behind.insert(0, back_through(i, behind[0]))
        g_total = behind[0]
        behind = behind[1:]
    ggroup[...] = g_total.astype(BF16)
    copies = [
        go(remote(ggroup, gz1, at(y1, g))),
        go(remote(ggroup, gz2, at(y2, g))),
    ]
    behind_me = pick(behind, x)
    for h in both_cores:
        dP[h] = mm3(dO[h], U[h], NT) * low_eq[h]
        dQ[h] = carried[h] * mm3(dO[h], state[h], NT) + mm3(dP[h], K[h])
        dK0[h] = mm3(dP[h], Q[h], TN)
        grad = nq[h] * (dQ[h] - Q[h] * jnp.sum(Q[h] * dQ[h], axis=1, keepdims=True))
        grad_pair[h, :, :N] = grad.astype(BF16)
    out_copy.wait_recv()
    head_outs = [
        pltpu.make_async_copy(
            out_heads.at[h], both_out.at[0, :, pl.ds(h * N, N)], local_sem.at[12 + h]
        )
        for h in range(C)
    ]
    for copy in head_outs:
        copy.start()
    next_copy.wait_recv()
    for copy in copies:
        copy.wait_recv()
    d_group = gz1[...].astype(F32) + dot(a_next[...], gz2[...], TN)
    d_chip = behind_me + mm3(after_me, d_group, TN)
    d_state = (ask[1] + mm3(A[1], d_chip, TN), d_chip)

    for h in both_cores:
        dX = dX0[h] + mm3(Y[h], d_state[h])
        both = mm3(dX, jnp.concatenate([U[h], state[h]], axis=0), NT)
        dL = -both[:, :F] * low[h]
        dG = beta[h] * dL
        dK = dK0[h] + mm3(final[h] * U[h], d_state[h], NT)
        dK = dK - carried[h] * beta[h] * both[:, F:]
        dK = dK + mm3(dG, K[h]) + mm3(dG, K[h], TN)
        d_beta = jnp.sum(dX * Zv[h], axis=1, keepdims=True)
        d_beta = d_beta + jnp.sum(dL * Gm[h], axis=1, keepdims=True)
        grad = nk[h] * (dK - K[h] * jnp.sum(K[h] * dK, axis=1, keepdims=True))
        d_logit = d_beta * beta[h] * (1.0 - sig[h])
        grad_pair[h, :, N : 2 * N] = grad.astype(BF16)
        grad_pair[h, :, 2 * N : 3 * N] = (beta[h] * dX).astype(BF16)
        grad_pair[h, :, 3 * N :] = jnp.broadcast_to(d_logit, (F, N)).astype(BF16)
    copy = go(remote(grad_pair.at[other], grad_heads.at[core], sibling))
    grad_heads[core] = grad_pair[core]
    copy.wait_recv()
    wide = [
        jnp.concatenate([grad_heads[h, :, i * N : (i + 1) * N] for h in range(C)], axis=1)
        for i in range(3)
    ]
    dlog = [grad_heads[h, :, 3 * N : 3 * N + 1].astype(F32) for h in range(C)]

    def partial(owner):
        here = pl.ds(pl.multiple_of(owner * W, W), W)
        rows = w_beta[:, here].astype(F32)
        value = dlog[0] * rows[0:1, :] + dlog[1] * rows[1:2, :]
        for i, weight in enumerate((wq, wk, wv)):
            value = value + dot(wide[i], weight[here, :], NT)
        return value

    hop = (-1, 1, -2, 2, -1, 1, -2, 2)
    parts = {}

    chunks = ((0, 16), (16, half), (half, F))

    def send_rows(kind, b, value):
        rows = pl.ds(chunks[b][0], chunks[b][1] - chunks[b][0])
        src, dst = rs_send.at[kind, rows], rs_recv.at[kind, rows]
        if kind in (2, 3):
            src, dst = src.at[:, pl.ds(0, N)], dst.at[:, pl.ds(0, N)]
            rs_send[kind, rows, :N] = value.astype(BF16)
        else:
            rs_send[kind, rows] = value.astype(BF16)
        reduces[kind, b] = go(remote(src, dst, along(hop[kind])))

    def rows_of(k, b):
        return parts[k][chunks[b][0] : chunks[b][1], :]

    def received(kind, b):
        reduces[kind, b].wait_recv()
        return rs_recv[kind, chunks[b][0] : chunks[b][1], :]

    reduces = {}
    for k, kinds in ((-3, (0,)), (3, (1,)), (4, (2, 3)), (-1, (4,)), (1, (5,))):
        parts[k] = partial(ring(k))
        for b in range(3):
            for kind in kinds:
                value = rows_of(k, b)
                if k == 4:
                    value = value[:, :N] if kind == 2 else value[:, N:]
                send_rows(kind, b, value)
    for k in (-2, 2, 0):
        parts[k] = partial(ring(k))

    def hand_on(b):
        for kind, k in ((6, -2), (7, 2)):
            value = rows_of(k, b) + received(kind - 6, b).astype(F32)
            extra = received(kind - 4, b)[:, :N].astype(F32)
            blank = jnp.zeros_like(extra)
            extra = jnp.concatenate([extra, blank] if kind == 6 else [blank, extra], axis=1)
            send_rows(kind, b, value + extra)

    def finish_rows(b):
        value = rows_of(0, b)
        for kind in (4, 5, 6, 7):
            value = value + received(kind, b).astype(F32)
        summed[chunks[b][0] : chunks[b][1], :] = value.astype(BF16)

    for b in range(3):
        hand_on(b)
    for b in range(3):
        finish_rows(b)
        if b == 0:
            halo = go(remote(summed.at[pl.ds(0, 16)], follow, (lax.rem(seq + S - 1, S), y)))
    ahead = pos_col + delay
    reaches = (ahead < S * F) & (clip_start(clip_lengths, ahead) <= pos_col)
    wanted = jnp.where(reaches, ahead - first, -1)
    pull = one_hot(wanted == iota((F, F + 16), 1))
    halo.wait_recv()
    both = jnp.concatenate([summed[...], follow[...]], axis=0)
    summed_out[...] = dot(pull, both).astype(BF16)
    last_out = pltpu.make_async_copy(summed_out, both_out.at[1], local_sem.at[11])
    last_out.start()
    for copy in started:
        copy.wait_send()
    for copy in head_outs:
        copy.wait()
    last_out.wait()


def on_device(
    dims,
    loaded,
    out_grad,
    w_query,
    w_key,
    w_value,
    w_beta,
    beta_max,
    out_gain,
    clip_lengths,
    delay_offsets,
    block_order,
):
    Z, X, H = dims["Z"], dims["X"], dims["H"]
    F, W = dims["F"], dims["W"]
    G = X * CORES
    BR = F // (Z * G)
    N = 128
    count = 128
    anyw = pl.BlockSpec(memory_space=pl.ANY)
    D = w_query.shape[0]
    scratch = [
        pltpu.VMEM((F, W), BF16),
        pltpu.VMEM((2, D), BF16),
        pltpu.SMEM(beta_max.shape, F32),
        pltpu.VMEM((1, N), F32),
        pltpu.SMEM(clip_lengths.shape, jnp.int32),
        pltpu.SMEM(delay_offsets.shape, jnp.int32),
        pltpu.VMEM(block_order.shape, jnp.int32),
        pltpu.VMEM((D, W), BF16),
        pltpu.VMEM((D, W), BF16),
        pltpu.VMEM((D, W), BF16),
        pltpu.VMEM((2, F, N), BF16),
        pltpu.VMEM((G, Z * BR, W), BF16),
        pltpu.VMEM((G, Z * BR, W), BF16),
        pltpu.VMEM((Z, G * BR, W), BF16),
        pltpu.VMEM((Z, G * BR, W), BF16),
        pltpu.VMEM((16, W), BF16),
        pltpu.VMEM((16, W), BF16),
        pltpu.VMEM((H, F, W), BF16),
        pltpu.VMEM((F, 3 * W + 128), F32),
        pltpu.VMEM((2, F, 4 * N), F32),
        pltpu.VMEM((2, F, 4 * N), F32),
        pltpu.VMEM((X, N, 2 * N), BF16),
        pltpu.VMEM((N, 2 * N), BF16),
        pltpu.VMEM((N, 2 * N), BF16),
        pltpu.VMEM((N, N), BF16),
        pltpu.VMEM((N, N), BF16),
        pltpu.VMEM((2, F, N), BF16),
        pltpu.VMEM((2, F, N), BF16),
        pltpu.VMEM((X, N, N), BF16),
        pltpu.VMEM((N, N), BF16),
        pltpu.VMEM((N, N), BF16),
        pltpu.VMEM((N, N), BF16),
        pltpu.VMEM((2, F, 4 * N), BF16),
        pltpu.VMEM((2, F, 4 * N), BF16),
        pltpu.VMEM((8, F, W), BF16),
        pltpu.VMEM((8, F, W), BF16),
        pltpu.VMEM((F, W), BF16),
        pltpu.VMEM((16, W), BF16),
        pltpu.VMEM((F, W), BF16),
        pltpu.SemaphoreType.DMA((16,)),
        pltpu.SemaphoreType.DMA((count,)),
        pltpu.SemaphoreType.DMA((count,)),
    ]
    result = pl.pallas_call(
        functools.partial(kernel, dims),
        out_shape=jax.ShapeDtypeStruct((2, F, W), BF16),
        in_specs=[anyw] * 11,
        out_specs=anyw,
        scratch_shapes=scratch,
        compiler_params=pltpu.CompilerParams(
            collective_id=0, has_side_effects=True, vmem_limit_bytes=60 * 2**20
        ),
    )(
        loaded,
        out_grad,
        w_query,
        w_key,
        w_value,
        w_beta.T,
        beta_max,
        out_gain.reshape(1, -1),
        clip_lengths,
        delay_offsets,
        block_order,
    )
    return result[0], result[1]


def build(mesh, chips_x, frames):
    seq, head = mesh.shape["seq"], mesh.shape["head"]
    dims = dict(Z=seq // (chips_x * CORES), X=chips_x, H=head, F=frames, W=256)
    return jax.shard_map(
        functools.partial(on_device, dims),
        mesh=mesh,
        in_specs=(
            P("seq", "head"),
            P("seq", "head"),
            P(None, "head"),
            P(None, "head"),
            P(None, "head"),
            P(None, "head"),
            P("head"),
            P(),
            P(),
            P(),
            P("seq", None),
        ),
        out_specs=(P("seq", "head"), P("seq", "head")),
        check_vma=False,
    )


def solution(mesh):
    return build(mesh, CHIPS_X, 128)
```
